512 devices in a mesh: owner: 32 (over x, z), split: 16 (over y, core).
Axes of the slice: x: 4, y: 8, z: 8, core: 2. Of those that a mesh axis runs over, the one named last changes fastest.
Arguments:
- new_rows: bfloat16 [65536, 256], P(('owner', 'split')), may hold values from -6 to 6
- cluster_ids: int32 [65536], P(('owner', 'split')), may hold values from 0 to 255, as said below
- slot_of_cluster: int32 [256], replicated, may hold values from 0 to 255, as said below
- row_counts: int32 [32, 16, 8], P('owner', 'split'), may hold values from 1 to 1024, 2048 in all within a row
- resident: bfloat16 [32, 16, 2048, 256], P('owner', 'split'), may hold values from -6 to 6
Outputs:
- max_cos: float32 [65536], P(('owner', 'split'))
- centroids: float32 [256, 256], P('owner')
The draws below stay inside these ranges and needn't reach their ends.
Inputs may be any that keep to these rules, and one draw needn't show every extreme that they name: `slot_of_cluster`: A permutation of the 256 slots. `cluster_ids`: the new rows of one device name clusters of at most 8 rows per owner group; for each index of split, one owner group gets exactly 8 rows from every device of that split index. `row_counts`: each device's counts sum to 2048.
All inputs are finite; a program needn't handle non-finite values.
Results may differ from the reference program's by a relative error of at most 0.0003.
Values may be sent and summed in bfloat16 or wider, within the bound.
A program may use at most 64 MiB of HBM per device.

```python
import math
import jax
import jax.numpy as jnp
import numpy as np
from jax import lax

EMB = 256
CL_OWN = 8
NEW_DEV = 128
RES_DEV = 2048
CAP = 8
CLUSTERS = 256
NEW_ROWS = 65536
N_OWNER = 32
N_SPLIT = 16


def route_tables(key):
    first_key, heavy_key, offset_key, order_key, member_key = jax.random.split(key, 5)
    slot_table = jax.random.permutation(first_key, CL_OWN * N_OWNER).astype(jnp.int32)
    cluster_at = jnp.argsort(slot_table).astype(jnp.int32)
    blocks = N_OWNER * N_SPLIT
    capacity = 2 * NEW_DEV // N_OWNER
    heavy_split = jax.random.randint(heavy_key, (N_SPLIT,), 0, N_OWNER).astype(jnp.int32)
    heavy_owner = jnp.tile(heavy_split, N_OWNER)[:, None]
    shift_value = jax.random.randint(offset_key, (blocks, 1), 0, N_OWNER - 1).astype(jnp.int32)
    column = jnp.arange(NEW_DEV, dtype=jnp.int32)[None, :]
    others = (heavy_owner + 1 + (column + shift_value) % (N_OWNER - 1)) % N_OWNER
    target = jnp.where(column < capacity, heavy_owner, others)
    scores = jax.random.randint(order_key, (blocks, NEW_DEV), 0, NEW_DEV).astype(jnp.int32) * NEW_DEV + column
    shuffle = jnp.argsort(scores, axis=1)
    target = jnp.take_along_axis(target, shuffle, axis=1)
    member = jax.random.randint(member_key, (blocks, NEW_DEV), 0, CL_OWN).astype(jnp.int32)
    cluster_list = cluster_at[(target * CL_OWN + member).reshape(-1)]
    return (slot_table, cluster_list.astype(jnp.int32))


def draw_slot_of_cluster(key, part):
    return route_tables(key)[0]


def draw_cluster_ids(key, part):
    return route_tables(key)[1]


def levels(own_key, dims, shards, smallest, high):
    def one(position, parts):
        heights = jax.random.uniform(jax.random.fold_in(jax.random.fold_in(own_key, 6), position), (parts,), jnp.float32, smallest / len(shards), high / len(shards))
        return jnp.repeat(jnp.exp(heights), dims[position] // parts).reshape((-1,) + (1,) * (len(dims) - position - 1))

    level = one(*shards[0])
    for cut in shards[1:]:
        level = level * one(*cut)
    return level


def length_profile(amount, total, reach, lean):
    weights = [(1 << 20) // math.isqrt(rank ** lean) + 1 for rank in range(2, amount + 1)]
    rest, counts = total - reach - (amount - 1), [1] * (amount - 1)
    while rest > 0:
        candidates = [i for i in range(amount - 1) if counts[i] < reach]
        pool, remaining = sum([weights[i] for i in candidates]), rest
        for i in candidates:
            more = min(reach - counts[i], max(1, remaining * weights[i] // pool), rest)
            counts[i] = counts[i] + more
            rest = rest - more
    return np.array([reach] + counts)


def ragged(key, number_of, total, most, lean):
    if number_of == 2:
        one = jax.random.randint(key, (), max(1, total - most), min(most, total - 1) + 1)
        return jnp.stack([one, total - one])
    lengths = jnp.asarray(length_profile(number_of, total, most, lean), jnp.int32)
    pairs = (number_of - 1) // 2
    source_of, taker = lengths[1:1 + 2 * pairs:2], lengths[2:2 + 2 * pairs:2]
    margin = jnp.minimum(source_of - 1, most - taker)
    moved = jax.random.randint(jax.random.fold_in(key, 1), (pairs,), 0, 1 << 20) % (margin + 1)
    lengths = lengths.at[1:1 + 2 * pairs:2].set(source_of - moved).at[2:2 + 2 * pairs:2].set(taker + moved)
    return lengths[jax.random.permutation(jax.random.fold_in(key, 2), number_of)]


def normal_values(own_key, dims, scale, bound, cuts=(), kind=jnp.bfloat16):
    array = jax.random.normal(own_key, dims, jnp.float32) * scale
    if len(cuts) > 0:
        array = levels(own_key, dims, cuts, -0.22, 0.18) * array
    return jnp.clip(array, min=-bound, max=bound).astype(kind)


def setup_inputs(seed: int = 0) -> dict:
    arg_keys = jax.random.split(jax.random.key(seed), 6)
    return {
        "new_rows": normal_values(arg_keys[0], (NEW_ROWS, EMB), 1.0, 6.0, ((0, 512),)),
        "cluster_ids": draw_cluster_ids(jax.random.fold_in(arg_keys[5], 71), 0),
        "slot_of_cluster": draw_slot_of_cluster(jax.random.fold_in(arg_keys[5], 71), 0),
        "row_counts": jax.vmap(lambda own: ragged(own, CL_OWN, RES_DEV, RES_DEV // 2, 2))(jax.random.split(arg_keys[3], N_OWNER * N_SPLIT)).reshape((N_OWNER, N_SPLIT, CL_OWN)).astype(jnp.int32),
        "resident": normal_values(arg_keys[4], (N_OWNER, N_SPLIT, RES_DEV, EMB), 1.0, 6.0, ((0, 32), (1, 16))),
    }


def scale_rows(values):
    floats = values.astype(jnp.float32)
    return lax.rsqrt(lax.optimization_barrier(jnp.sum(floats * floats, axis=-1)) + 1e-06)

def unit_rows(values):
    return values.astype(jnp.float32) * scale_rows(values)[..., None]

def lookup(indices, small_table):
    match = indices[:, None] == jnp.arange(small_table.shape[0], dtype=jnp.int32)[None, :]
    return lax.optimization_barrier(jnp.sum(jnp.where(match, small_table[None, :], 0), axis=1)).astype(jnp.int32)

def reference(new_rows, cluster_ids, slot_of_cluster, row_counts, resident):
    slot = slot_of_cluster[cluster_ids].astype(jnp.int32)
    target = (slot // CL_OWN).astype(jnp.int32)
    member = (slot % CL_OWN).astype(jnp.int32)
    order = jnp.argsort(target, stable=True)
    sorted_target = target[order]
    first_place = jnp.searchsorted(sorted_target, sorted_target, side='left').astype(jnp.int32)
    rank = jnp.zeros_like(target).at[order].set(jnp.arange(NEW_ROWS, dtype=jnp.int32) - first_place)
    queue_len = N_OWNER * N_SPLIT * CAP
    query_buffer = jnp.zeros((N_OWNER, queue_len, EMB), jnp.bfloat16).at[target, rank].set(new_rows)
    member_buffer = jnp.full((N_OWNER, queue_len), -1, jnp.int32).at[target, rank].set(member)
    row_end = jnp.cumsum(row_counts, axis=-1).astype(jnp.int32)
    row_begin = (row_end - row_counts).astype(jnp.int32)

    def per_owner(owner_index):
        queries = query_buffer[owner_index]
        members = member_buffer[owner_index]
        inv_query = scale_rows(queries)

        def per_split(split_index):
            held_rows = resident[owner_index, split_index]
            inv_held = scale_rows(held_rows)
            ends = row_end[owner_index, split_index]
            begins = row_begin[owner_index, split_index]
            inner = jnp.dot(queries, held_rows.T, preferred_element_type=jnp.float32) * inv_held[None, :]
            low = lookup(members, begins)
            high = lookup(members, ends)
            row_index = jnp.arange(RES_DEV, dtype=jnp.int32)[None, :]
            inside = (row_index >= low[:, None]) & (row_index < high[:, None])
            found_max = lax.optimization_barrier(jnp.max(jnp.where(inside, inner, -3.0), axis=1))
            row_cluster = lax.optimization_barrier(jnp.sum((jnp.arange(RES_DEV, dtype=jnp.int32)[:, None] >= ends[None, :]).astype(jnp.int32), axis=1))
            weights = (row_cluster[None, :] == jnp.arange(CL_OWN, dtype=jnp.int32)[:, None]).astype(jnp.float32)
            held_sum = jnp.dot(weights, held_rows.astype(jnp.float32) * inv_held[:, None], precision=lax.Precision.HIGHEST)
            return (found_max, held_sum)
        found_all, held_all = lax.map(per_split, jnp.arange(N_SPLIT, dtype=jnp.int32))
        return (lax.optimization_barrier(jnp.max(found_all, axis=0)) * inv_query, lax.optimization_barrier(jnp.sum(held_all, axis=0)))
    maxima, held_sums = lax.map(per_owner, jnp.arange(N_OWNER, dtype=jnp.int32))
    max_cos = maxima[target, rank]
    new_sums = jax.ops.segment_sum(unit_rows(new_rows), slot, num_segments=CLUSTERS)
    cluster_sum = held_sums.reshape(CLUSTERS, EMB) + new_sums
    return (max_cos, unit_rows(cluster_sum))
```

```python
import functools

import jax
import jax.numpy as jnp
from jax import lax
from jax.experimental import pallas as pl
from jax.experimental.pallas import tpu as pltpu
from jax.sharding import PartitionSpec as P

F32, BF16, I32 = jnp.float32, jnp.bfloat16, jnp.int32
MESH = pl.DeviceIdType.MESH
NT = (((1,), (1,)), ((), ()))
NN = (((1,), (0,)), ((), ()))
EPS = 1e-06
LOWEST = -3.0


def iota(shape, dim):
    return lax.broadcasted_iota(I32, shape, dim)


def mm(lhs, rhs, dims=NN):
    return lax.dot_general(lhs, rhs, dims, preferred_element_type=F32)


def column_to_row(column):
    pieces = []
    for start in range(0, column.shape[0], 128):
        piece = column[start : start + 128]
        n = piece.shape[0]
        wide = jnp.broadcast_to(piece, (n, n))
        eye = iota((n, n), 0) == iota((n, n), 1)
        pieces.append(jnp.sum(jnp.where(eye, wide, 0.0), axis=0, keepdims=True))
    return pieces[0] if len(pieces) == 1 else jnp.concatenate(pieces, axis=1)


def split_weights(mask, row):
    high = row.astype(BF16).astype(F32)
    low = row - high
    return jnp.concatenate(
        [jnp.where(mask, high, 0.0), jnp.where(mask, low, 0.0)], axis=0
    ).astype(BF16)


def kernel(
    dims,
    ids_ref,
    table_ref,
    counts_ref,
    rows_ref,
    resident_ref,
    max_ref,
    cent_ref,
    held,
    scale_col,
    cluster_col,
    send_rows,
    send_members,
    got_rows,
    got_members,
    blocks,
    members,
    part,
    part_got,
    total_own,
    total,
    best_own,
    best_got,
    ret_own,
    ret_got,
    load_sem,
    sems,
    major_send,
    major_recv,
    minor_send,
    minor_recv,
    sib_send,
    sib_recv,
):
    owners, splits, local, width, clusters, res_rows, cap = dims
    slots = owners * cap
    half = slots // 2
    lane_group = min(128, slots)
    groups = slots // lane_group
    owners_in_group = lane_group // cap
    chunk = clusters * width // splits
    chunks_in_row = width // chunk
    ny = splits // 2
    me_o = lax.axis_index("owner")
    me_s = lax.axis_index("split")
    y = me_s // 2
    core = me_s - 2 * y
    step_dir = 1 - 2 * core
    sibling = 2 * y + 1 - core

    def at_y(offset):
        return 2 * lax.rem(y + offset * step_dir + 4 * ny, ny) + core

    def sib_at_y(offset):
        return 2 * lax.rem(y - offset * step_dir + 4 * ny, ny) + 1 - core

    def other_owner(k):
        return lax.rem(me_o + k, owners)

    def other_split(k):
        return lax.rem(me_s + k, splits)

    def remote(src, dst, send, recv, owner, split):
        return pltpu.make_async_remote_copy(
            src_ref=src,
            dst_ref=dst,
            send_sem=send,
            recv_sem=recv,
            device_id=(owner, split),
            device_id_type=MESH,
        )

    def wait_all(ref, count, kind, side):
        piece = ref.at[pl.ds(0, count)]
        pltpu.make_async_copy(piece, piece, sems.at[kind, side]).wait()

    ROWS, MEMBERS, GATHER, PART, TOTAL, BEST, RET = range(7)

    load = pltpu.make_async_copy(resident_ref, held, load_sem)
    load.start()

    barrier = pltpu.get_barrier_semaphore()

    @pl.loop(1, owners)
    def _(k):
        pl.semaphore_signal(
            barrier, inc=1, device_id=(other_owner(k), me_s), device_id_type=MESH
        )

    @pl.loop(1, splits)
    def _(k):
        pl.semaphore_signal(
            barrier, inc=1, device_id=(me_o, other_split(k)), device_id_type=MESH
        )

    ids = ids_ref[...]
    count_of_clusters = table_ref.shape[1]
    hot = jnp.where(iota((count_of_clusters, local), 0) == ids, 1.0, 0.0).astype(BF16)
    table = jnp.broadcast_to(table_ref[...].astype(F32), (8, count_of_clusters)).astype(BF16)
    slot = mm(table, hot)[0:1].astype(I32)
    target = lax.div(slot, clusters)
    member = slot - target * clusters
    target_hot = jnp.where(iota((owners, local), 0) == target, 1.0, 0.0)
    earlier = jnp.where(iota((local, local), 0) < iota((local, local), 1), 1.0, 0.0).astype(BF16)
    before = mm(target_hot.astype(BF16), earlier)
    place = jnp.sum(target_hot * before, axis=0, keepdims=True).astype(I32)
    flat = target * cap + place
    rows = rows_ref[...]
    scatter = jnp.where(iota((slots, local), 0) == flat, 1.0, 0.0).astype(BF16)
    send_rows[...] = mm(scatter, rows).reshape(owners, cap, width).astype(BF16)
    target_member = (target_hot * (member + 1).astype(F32)).astype(BF16)
    place_hot = jnp.where(
        lax.rem(iota((lane_group, local), 0), cap) == place, 1.0, 0.0
    ).astype(BF16)
    member_rows = mm(target_member, place_hot, NT)
    for o in range(owners):
        send_members[o] = member_rows[o : o + 1]

    pl.semaphore_wait(barrier, owners + splits - 2)

    @pl.loop(1, owners)
    def _(k):
        o = other_owner(k)
        remote(
            send_members.at[o],
            got_members.at[me_o],
            sems.at[MEMBERS, 0],
            sems.at[MEMBERS, 1],
            o,
            me_s,
        ).start()
        remote(
            send_rows.at[o],
            got_rows.at[me_o],
            sems.at[ROWS, 0],
            sems.at[ROWS, 1],
            o,
            me_s,
        ).start()

    got_rows[me_o] = send_rows[me_o]
    got_members[me_o] = send_members[me_o]

    floats = rows.astype(F32)
    own_scale = lax.rsqrt(
        column_to_row(jnp.sum(floats * floats, axis=1, keepdims=True)) + EPS
    )
    ends = []
    running = counts_ref[0, 0]
    for j in range(clusters):
        ends.append(running)
        if j + 1 < clusters:
            running = running + counts_ref[0, j + 1]
    load.wait()
    step_rows = 256

    def cluster_of(index):
        result = jnp.ones(index.shape, I32)
        for end in ends[:-1]:
            result = result + jnp.where(index >= end, 1, 0)
        return result

    def held_step(t, acc):
        start = pl.multiple_of(t * step_rows, step_rows)
        x = held[pl.ds(start, step_rows)]
        f = x.astype(F32)
        scale = lax.rsqrt(jnp.sum(f * f, axis=1, keepdims=True) + EPS)
        scale_col[pl.ds(start, step_rows)] = jnp.broadcast_to(scale, (step_rows, 128))
        cluster_col[pl.ds(start, step_rows)] = cluster_of(
            iota((step_rows, 128), 0) + start
        ).astype(F32)
        row = column_to_row(scale)
        mask = cluster_of(iota((clusters, step_rows), 1) + start) == iota(
            (clusters, step_rows), 0
        ) + 1
        return acc + mm(split_weights(mask, row), x)

    held_sum = lax.fori_loop(
        0, res_rows // step_rows, held_step, jnp.zeros((2 * clusters, width), F32)
    )

    wait_all(got_members, owners - 1, MEMBERS, 1)
    pieces = []
    for g in range(groups):
        owner_of_lane = lax.div(iota((1, lane_group), 1), cap) + g * owners_in_group
        acc = jnp.zeros((1, lane_group), F32)
        for o in range(g * owners_in_group, (g + 1) * owners_in_group):
            acc = acc + jnp.where(owner_of_lane == o, got_members[o], 0.0)
        pieces.append(acc)
    own_members = pieces[0] if groups == 1 else jnp.concatenate(pieces, axis=1)
    members[me_s] = own_members

    @pl.loop(1, splits)
    def _(k):
        s = other_split(k)
        remote(
            members.at[me_s],
            members.at[me_s],
            sems.at[GATHER, 0],
            sems.at[GATHER, 1],
            me_o,
            s,
        ).start()

    wait_all(got_rows, owners - 1, ROWS, 1)
    own_block = got_rows[...].astype(F32).reshape(slots, width)
    for h in range(2):
        blocks[2 * me_s + h] = own_block[h * half : (h + 1) * half].astype(BF16)

    last_major, last_minor = ny // 2, ny // 2 - 1
    up, down = at_y(1), at_y(-1)

    def major(k, h):
        slot_ref = blocks.at[2 * at_y(1 - k) + h]
        return remote(slot_ref, slot_ref, major_send.at[k - 1, h], major_recv.at[k - 1, h], me_o, up)

    def minor(k, h):
        slot_ref = blocks.at[2 * at_y(k - 1) + h]
        return remote(slot_ref, slot_ref, minor_send.at[k - 1, h], minor_recv.at[k - 1, h], me_o, down)

    def to_sibling(index, offset, h):
        slot_ref = blocks.at[2 * at_y(offset) + h]
        return remote(slot_ref, slot_ref, sib_send.at[index, h], sib_recv.at[index, h], me_o, sibling)

    def major_arrived(k, h):
        slot_ref = blocks.at[2 * at_y(-k) + h]
        remote(slot_ref, slot_ref, major_send.at[k - 1, h], major_recv.at[k - 1, h], me_o, up).wait_recv()

    def minor_arrived(k, h):
        slot_ref = blocks.at[2 * at_y(k) + h]
        remote(slot_ref, slot_ref, minor_send.at[k - 1, h], minor_recv.at[k - 1, h], me_o, down).wait_recv()

    def sibling_arrived(index, offset):
        for h in range(2):
            slot_ref = blocks.at[2 * sib_at_y(offset) + h]
            remote(
                slot_ref, slot_ref, sib_send.at[index, h], sib_recv.at[index, h], me_o, sibling
            ).wait_recv()

    for h in range(2):
        if last_major:
            major(1, h).start()
        if last_minor:
            minor(1, h).start()
        to_sibling(0, 0, h).start()

    def score(s):
        queries = blocks[pl.ds(2 * s, 2)].reshape(slots, width)
        wanted = members[s]
        score_rows = min(512, res_rows)

        def step(t, best):
            start = pl.multiple_of(t * score_rows, score_rows)
            inner = mm(held[pl.ds(start, score_rows)], queries, NT)
            kept = []
            for g in range(groups):
                lanes = slice(g * lane_group, (g + 1) * lane_group)
                value = inner[:, lanes] * scale_col[pl.ds(start, score_rows)][:, :lane_group]
                inside = cluster_col[pl.ds(start, score_rows)][:, :lane_group] == wanted[:, lanes]
                value = jnp.where(inside, value, LOWEST)
                kept.append(jnp.max(value.reshape(score_rows // 8, 8, lane_group), axis=0))
            new = kept[0] if groups == 1 else jnp.concatenate(kept, axis=1)
            return jnp.maximum(best, new)

        best = lax.fori_loop(
            0, res_rows // score_rows, step, jnp.full((8, slots), LOWEST, F32)
        )
        return jnp.max(best, axis=0, keepdims=True)

    def score_and_send(s):
        best_own[s] = score(s)
        remote(
            best_own.at[s],
            best_got.at[me_s],
            sems.at[BEST, 0],
            sems.at[BEST, 1],
            me_o,
            s,
        ).start()

    block_scale = lax.rsqrt(
        column_to_row(jnp.sum(own_block * own_block, axis=1, keepdims=True)) + EPS
    )
    new_mask = jnp.broadcast_to(own_members, (clusters, slots)) == (
        iota((clusters, slots), 0) + 1
    ).astype(F32)
    both = held_sum + mm(split_weights(new_mask, block_scale), own_block.astype(BF16))
    partial = both[:clusters] + both[clusters:]
    for s in range(splits):
        row, lane = s // chunks_in_row, (s % chunks_in_row) * chunk
        part[s] = partial[row : row + 1, lane : lane + chunk]

    @pl.loop(1, splits)
    def _(k):
        s = other_split(k)
        remote(
            part.at[s], part_got.at[me_s], sems.at[PART, 0], sems.at[PART, 1], me_o, s
        ).start()

    part_got[me_s] = part[me_s]

    wait_all(members, splits - 1, GATHER, 1)
    best_got[me_s] = score(me_s)

    for k in range(1, last_major + 1):
        for h in range(2):
            major_arrived(k, h)
            if k < last_major:
                major(k + 1, h).start()
            to_sibling(k, -k, h).start()
            if k <= last_minor:
                minor_arrived(k, h)
                if k < last_minor:
                    minor(k + 1, h).start()
                to_sibling(last_major + k, k, h).start()
            if h == 0:
                if k == 1:
                    sibling_arrived(0, 0)
                    score_and_send(sib_at_y(0))
                else:
                    sibling_arrived(k - 1, -(k - 1))
                    score_and_send(sib_at_y(-(k - 1)))
                    sibling_arrived(last_major + k - 1, k - 1)
                    score_and_send(sib_at_y(k - 1))
        score_and_send(at_y(-k))
        if k <= last_minor:
            score_and_send(at_y(k))
        if k == 1:
            wait_all(part_got, splits - 1, PART, 1)
            total_own[...] = jnp.sum(part_got[...], axis=0)

            @pl.loop(1, splits)
            def _(j):
                remote(
                    total_own, total.at[me_s], sems.at[TOTAL, 0], sems.at[TOTAL, 1], me_o, other_split(j)
                ).start()

            total[me_s] = total_own[...]
    sibling_arrived(last_major, -last_major)
    score_and_send(sib_at_y(-last_major))

    wait_all(total, splits - 1, TOTAL, 1)
    summed = []
    for j in range(clusters):
        bits = [total[j * chunks_in_row + i] for i in range(chunks_in_row)]
        summed.append(bits[0] if chunks_in_row == 1 else jnp.concatenate(bits, axis=1))
    for j in range(clusters):
        v = summed[j]
        cent_ref[j : j + 1] = v * lax.rsqrt(jnp.sum(v * v, axis=1, keepdims=True) + EPS)

    wait_all(best_got, splits - 1, BEST, 1)
    best = jnp.max(best_got[...], axis=0)
    for g in range(groups):
        ret_own[g] = best[:, g * lane_group : (g + 1) * lane_group]

    @pl.loop(1, owners)
    def _(k):
        o = other_owner(k)
        remote(
            ret_own.at[lax.div(o, owners_in_group)],
            ret_got.at[me_o],
            sems.at[RET, 0],
            sems.at[RET, 1],
            o,
            me_s,
        ).start()

    ret_got[me_o] = ret_own[lax.div(me_o, owners_in_group)]

    wait_all(send_rows, owners - 1, ROWS, 0)
    wait_all(send_members, owners - 1, MEMBERS, 0)
    wait_all(members, splits - 1, GATHER, 0)
    wait_all(part, splits - 1, PART, 0)
    wait_all(total, splits - 1, TOTAL, 0)
    wait_all(best_own, splits - 1, BEST, 0)
    for h in range(2):
        for k in range(1, last_major + 1):
            major(k, h).wait_send()
            to_sibling(k, -k, h).wait_send()
        for k in range(1, last_minor + 1):
            minor(k, h).wait_send()
            to_sibling(last_major + k, k, h).wait_send()
        to_sibling(0, 0, h).wait_send()

    wait_all(ret_got, owners - 1, RET, 1)
    lane_of_row = lax.rem(me_o, owners_in_group) * cap + place
    lane_hot = iota((lane_group, local), 0) == lane_of_row
    table_rows = jnp.concatenate([ret_got[o] for o in range(owners)], axis=0)
    high = table_rows.astype(BF16).astype(F32)
    mid = (table_rows - high).astype(BF16).astype(F32)
    low = table_rows - high - mid
    stacked = jnp.concatenate([high, mid, low], axis=0).astype(BF16)
    picked = mm(stacked, jnp.where(lane_hot, 1.0, 0.0).astype(BF16))
    picked = picked[:owners] + picked[owners : 2 * owners] + picked[2 * owners :]
    max_ref[...] = own_scale * jnp.sum(target_hot * picked, axis=0, keepdims=True)
    wait_all(ret_got, owners - 1, RET, 0)


def body(new_rows, cluster_ids, slot_of_cluster, row_counts, resident):
    owners, splits = lax.axis_size("owner"), lax.axis_size("split")
    local, width = new_rows.shape
    clusters = row_counts.shape[2]
    res_rows = resident.shape[2]
    cap = 2 * local // owners
    slots = owners * cap
    half = slots // 2
    lane_group = min(128, slots)
    chunk = clusters * width // splits
    ny = splits // 2
    vmem = pl.BlockSpec(memory_space=pltpu.VMEM)
    dma = pltpu.SemaphoreType.DMA
    best, centroids = pl.pallas_call(
        functools.partial(kernel, (owners, splits, local, width, clusters, res_rows, cap)),
        out_shape=(
            jax.ShapeDtypeStruct((1, local), F32),
            jax.ShapeDtypeStruct((clusters, width), F32),
        ),
        in_specs=[
            vmem,
            vmem,
            pl.BlockSpec(memory_space=pltpu.SMEM),
            vmem,
            pl.BlockSpec(memory_space=pl.ANY),
        ],
        out_specs=(vmem, vmem),
        scratch_shapes=[
            pltpu.VMEM((res_rows, width), BF16),
            pltpu.VMEM((res_rows, 128), F32),
            pltpu.VMEM((res_rows, 128), F32),
            pltpu.VMEM((owners, cap, width), BF16),
            pltpu.VMEM((owners, 1, lane_group), F32),
            pltpu.VMEM((owners, cap, width), BF16),
            pltpu.VMEM((owners, 1, lane_group), F32),
            pltpu.VMEM((2 * splits, half, width), BF16),
            pltpu.VMEM((splits, 1, slots), F32),
            pltpu.VMEM((splits, 1, chunk), F32),
            pltpu.VMEM((splits, 1, chunk), F32),
            pltpu.VMEM((1, chunk), F32),
            pltpu.VMEM((splits, 1, chunk), F32),
            pltpu.VMEM((splits, 1, slots), F32),
            pltpu.VMEM((splits, 1, slots), F32),
            pltpu.VMEM((slots // lane_group, 1, lane_group), F32),
            pltpu.VMEM((owners, 1, lane_group), F32),
            dma,
            dma((7, 2)),
            dma((max(1, ny // 2), 2)),
            dma((max(1, ny // 2), 2)),
            dma((max(1, ny // 2 - 1), 2)),
            dma((max(1, ny // 2 - 1), 2)),
            dma((ny, 2)),
            dma((ny, 2)),
        ],
        compiler_params=pltpu.CompilerParams(
            collective_id=0, has_side_effects=True, vmem_limit_bytes=48 * 1024 * 1024
        ),
        cost_estimate=pl.CostEstimate(
            flops=2 * splits * slots * res_rows * width, bytes_accessed=4 << 20, transcendentals=0
        ),
    )(
        cluster_ids.reshape(1, -1),
        slot_of_cluster.reshape(1, -1),
        row_counts.reshape(1, -1),
        new_rows,
        resident.reshape(res_rows, width),
    )
    return best.reshape(-1), centroids


def solution(mesh):
    placed = (
        P(("owner", "split"), None),
        P(("owner", "split")),
        P(),
        P("owner", "split", None),
        P("owner", "split", None, None),
    )
    return jax.shard_map(
        body,
        mesh=mesh,
        in_specs=placed,
        out_specs=(P(("owner", "split")), P("owner", None)),
        check_vma=False,
    )
```

```python
import functools

import jax
import jax.numpy as jnp
from jax import lax
from jax.experimental import pallas as pl
from jax.experimental.pallas import tpu as pltpu
from jax.sharding import PartitionSpec as P

F32, BF16, I32 = jnp.float32, jnp.bfloat16, jnp.int32
MESH = pl.DeviceIdType.MESH
NT = (((1,), (1,)), ((), ()))
NN = (((1,), (0,)), ((), ()))
EPS = 1e-06
LOWEST = -3.0
PIECES = 4


def iota(shape, dim):
    return lax.broadcasted_iota(I32, shape, dim)


def mm(lhs, rhs, dims=NN):
    return lax.dot_general(lhs, rhs, dims, preferred_element_type=F32)


def column_to_row(column):
    pieces = []
    for start in range(0, column.shape[0], 128):
        piece = column[start : start + 128]
        n = piece.shape[0]
        wide = jnp.broadcast_to(piece, (n, n))
        eye = iota((n, n), 0) == iota((n, n), 1)
        pieces.append(jnp.sum(jnp.where(eye, wide, 0.0), axis=0, keepdims=True))
    return pieces[0] if len(pieces) == 1 else jnp.concatenate(pieces, axis=1)


def split_weights(mask, row):
    high = row.astype(BF16).astype(F32)
    low = row - high
    return jnp.concatenate(
        [jnp.where(mask, high, 0.0), jnp.where(mask, low, 0.0)], axis=0
    ).astype(BF16)


def displacements(owners):
    across = 4 if owners == 32 else 1
    along = owners // across

    def hops(d):
        return min(d[0], across - d[0]) + min(d[1], along - d[1])

    near = sorted(((dx, dz) for dx in range(across) for dz in range(along)), key=hops)
    return across, along, near


def kernel(
    dims,
    ids_hbm,
    table_hbm,
    counts_hbm,
    rows_hbm,
    resident_hbm,
    max_ref,
    cent_ref,
    ids_ref,
    table_ref,
    counts_ref,
    rows_ref,
    held,
    scale_col,
    cluster_col,
    send_rows,
    send_members,
    got_rows,
    got_members,
    blocks,
    members,
    held_sums,
    part,
    part_got,
    total_own,
    total,
    best_own,
    best_got,
    ret_own,
    ret_got,
    load_sems,
    piece_sems,
    sems,
    major_send,
    major_recv,
    minor_send,
    minor_recv,
    sib_send,
    sib_recv,
):
    owners, splits, local, width, clusters, res_rows, cap = dims
    across, along, near = displacements(owners)
    slots = owners * cap
    lane_group = min(128, slots)
    groups = slots // lane_group
    owners_in_group = lane_group // cap
    piece_owners = owners // PIECES
    piece_rows = slots // PIECES
    chunk = clusters * width // splits
    chunks_in_row = width // chunk
    ny = splits // 2
    last_major, last_minor = ny // 2, ny // 2 - 1
    me_o = lax.axis_index("owner")
    me_s = lax.axis_index("split")
    me_x, me_z = me_o // along, me_o % along
    y = me_s // 2
    core = me_s - 2 * y
    step_dir = 1 - 2 * core
    sibling = 2 * y + 1 - core

    def at_y(offset):
        return 2 * ((y + offset * step_dir + 4 * ny) % ny) + core

    def target_of(r):
        dx, dz = near[r]
        return ((me_x + across - dx) % across) * along + (me_z + along - dz) % along

    def source_of(r):
        dx, dz = near[r]
        return ((me_x + dx) % across) * along + (me_z + dz) % along

    def other_split(k):
        return (me_s + k) % splits

    def remote(src, dst, send, recv, owner, split):
        return pltpu.make_async_remote_copy(
            src_ref=src,
            dst_ref=dst,
            send_sem=send,
            recv_sem=recv,
            device_id=(owner, split),
            device_id_type=MESH,
        )

    def wait_piece(piece, sem):
        pltpu.make_async_copy(piece, piece, sem).wait()

    def wait_all(ref, count, kind, side):
        wait_piece(ref.at[pl.ds(0, count)], sems.at[kind, side])

    ROWS, MEMBERS, PART, TOTAL, BEST, RET = range(6)

    loads = [
        pltpu.make_async_copy(src, dst, load_sems.at[i])
        for i, (src, dst) in enumerate(
            (
                (ids_hbm, ids_ref),
                (table_hbm, table_ref),
                (rows_hbm, rows_ref),
                (counts_hbm, counts_ref),
                (resident_hbm, held),
            )
        )
    ]
    barrier = pltpu.get_barrier_semaphore()

    @pl.loop(1, owners)
    def _(k):
        pl.semaphore_signal(
            barrier, inc=1, device_id=((me_o + k) % owners, me_s), device_id_type=MESH
        )

    for load in loads:
        load.start()

    @pl.loop(1, splits)
    def _(k):
        pl.semaphore_signal(
            barrier, inc=1, device_id=(me_o, other_split(k)), device_id_type=MESH
        )

    loads[0].wait()
    loads[1].wait()
    ids = ids_ref[...]
    all_clusters = table_ref.shape[1]
    hot = jnp.where(iota((all_clusters, local), 0) == ids, 1.0, 0.0).astype(BF16)
    table = jnp.broadcast_to(table_ref[...].astype(F32), (8, all_clusters)).astype(BF16)
    slot = mm(table, hot)[0:1].astype(I32)
    target = lax.div(slot, clusters)
    member = slot - target * clusters
    order = iota((owners, local), 0)
    target_of_order = jnp.zeros((owners, local), I32)
    for r in range(owners):
        target_of_order = jnp.where(order == r, target_of(r), target_of_order)
    target_hot = jnp.where(target_of_order == target, 1.0, 0.0)
    rank = jnp.sum(target_hot * order.astype(F32), axis=0, keepdims=True).astype(I32)
    earlier = jnp.where(iota((local, local), 0) < iota((local, local), 1), 1.0, 0.0).astype(BF16)
    before = mm(target_hot.astype(BF16), earlier)
    place = jnp.sum(target_hot * before, axis=0, keepdims=True).astype(I32)
    flat = rank * cap + place
    target_member = (target_hot * (member + 1).astype(F32)).astype(BF16)
    place_hot = jnp.where(
        lax.rem(iota((lane_group, local), 0), cap) == place, 1.0, 0.0
    ).astype(BF16)
    member_rows = mm(target_member, place_hot, NT)
    for r in range(owners):
        send_members[r] = member_rows[r : r + 1]
    loads[2].wait()
    rows = rows_ref[...]
    scatter = jnp.where(iota((slots, local), 0) == flat, 1.0, 0.0).astype(BF16)
    send_rows[...] = mm(scatter, rows).reshape(owners, cap, width).astype(BF16)

    pl.semaphore_wait(barrier, owners + splits - 2)

    for r in range(owners - 1, 0, -1):
        remote(
            send_rows.at[r],
            got_rows.at[r],
            sems.at[ROWS, 0],
            piece_sems.at[r // piece_owners],
            target_of(r),
            me_s,
        ).start()
        remote(
            send_members.at[r],
            got_members.at[r],
            sems.at[MEMBERS, 0],
            sems.at[MEMBERS, 1],
            target_of(r),
            me_s,
        ).start()
    got_rows[0] = send_rows[0]
    got_members[0] = send_members[0]

    floats = rows.astype(F32)
    own_scale = lax.rsqrt(
        column_to_row(jnp.sum(floats * floats, axis=1, keepdims=True)) + EPS
    )
    loads[3].wait()
    loads[4].wait()
    ends = []
    running = counts_ref[0, 0]
    for j in range(clusters):
        ends.append(running)
        if j + 1 < clusters:
            running = running + counts_ref[0, j + 1]
    step_rows = 256

    def cluster_of(index):
        result = jnp.ones(index.shape, I32)
        for end in ends[:-1]:
            result = result + jnp.where(index >= end, 1, 0)
        return result

    def held_step(t, acc):
        start = pl.multiple_of(t * step_rows, step_rows)
        x = held[pl.ds(start, step_rows)]
        f = x.astype(F32)
        scale = lax.rsqrt(jnp.sum(f * f, axis=1, keepdims=True) + EPS)
        scale_col[pl.ds(start, step_rows)] = jnp.broadcast_to(scale, (step_rows, 128))
        cluster_col[pl.ds(start, step_rows)] = cluster_of(
            iota((step_rows, 128), 0) + start
        ).astype(F32)
        row = column_to_row(scale)
        mask = cluster_of(iota((clusters, step_rows), 1) + start) == iota(
            (clusters, step_rows), 0
        ) + 1
        return acc + mm(split_weights(mask, row), x)

    held_sums[...] = lax.fori_loop(
        0, res_rows // step_rows, held_step, jnp.zeros((2 * clusters, width), F32)
    )

    def piece_of(block, p):
        return members.at[block] if p == PIECES else blocks.at[PIECES * block + p]

    def up(block, k, p, hops=1):
        ref = piece_of(block, p)
        return remote(ref, ref, major_send.at[k - 1, p], major_recv.at[k - 1, p], me_o, at_y(hops))

    def down(block, k, p):
        ref = piece_of(block, p)
        return remote(ref, ref, minor_send.at[k - 1, p], minor_recv.at[k - 1, p], me_o, at_y(-1))

    def aside(block, index, p):
        ref = piece_of(block, p)
        return remote(ref, ref, sib_send.at[index, p], sib_recv.at[index, p], me_o, sibling)

    skip = ny == 8

    def skipped(p):
        return skip and p >= PIECES - 1

    def start_own(p):
        up(me_s, 1, p).start()
        if last_minor:
            down(me_s, 1, p).start()
        aside(me_s, 0, p).start()

    for p in range(PIECES):
        first = max(1, p * piece_owners)
        count = (p + 1) * piece_owners - first
        if count:
            wait_piece(got_rows.at[pl.ds(first, count)], piece_sems.at[p])
        blocks[PIECES * me_s + p] = (
            got_rows[pl.ds(p * piece_owners, piece_owners)]
            .astype(F32)
            .reshape(piece_rows, width)
            .astype(BF16)
        )
        start_own(p)
    wait_all(got_members, owners - 1, MEMBERS, 1)
    pieces = []
    for g in range(groups):
        order_of_lane = lax.div(iota((1, lane_group), 1), cap) + g * owners_in_group
        acc = jnp.zeros((1, lane_group), F32)
        for r in range(g * owners_in_group, (g + 1) * owners_in_group):
            acc = acc + jnp.where(order_of_lane == r, got_members[r], 0.0)
        pieces.append(acc)
    members[me_s] = pieces[0] if groups == 1 else jnp.concatenate(pieces, axis=1)
    start_own(PIECES)

    def handle(k, p):
        block = at_y(-k)
        up(block, k, p).wait_recv()
        if not skipped(p):

            @pl.when(k < last_major)
            def _():
                up(block, k + 1, p).start()

        else:

            @pl.when(k < 3)
            def _():
                up(block, k + 1, p).start()

            @pl.when(k == 2)
            def _():
                up(block, 4, p, hops=2).start()

        aside(block, 2 * k - 1, p).start()
        if last_minor:

            @pl.when(k <= last_minor)
            def _():
                block = at_y(k)
                down(block, k, p).wait_recv()

                @pl.when(k < last_minor)
                def _():
                    down(block, k + 1, p).start()

                aside(block, 2 * k, p).start()

    def handle_piece(k, p):
        handle(k, p)
        if p == PIECES - 1:
            handle(k, PIECES)

    def score_step(n, carry):
        k, j = (n + 2) // 4, (n + 2) % 4
        minor, other = j // 2, j % 2
        sign = (1 - 2 * minor) * (1 - 2 * other)
        block = 2 * ((y - sign * k * step_dir + 4 * ny) % ny) + core + other * step_dir

        @pl.when(n == 2)
        def _():
            for p in range(PIECES):
                handle_piece(1, p)

        if last_major > 1:
            t = n - 3
            for p in range(PIECES):

                @pl.when((n >= 3) & (n < 3 + 4 * (last_major - 1)) & (t % 4 == p))
                def _():
                    handle_piece(t // 4 + 2, p)

        @pl.when(other == 1)
        def _():
            for p in range(PIECES + 1):
                aside(block, n // 2, p).wait_recv()

        queries = blocks[pl.ds(PIECES * block, PIECES)].reshape(slots, width)
        wanted = members[block]
        inner = mm(held[...], queries, NT)
        kept = []
        for g in range(groups):
            lanes = slice(g * lane_group, (g + 1) * lane_group)
            value = inner[:, lanes] * scale_col[:, :lane_group]
            value = jnp.where(cluster_col[:, :lane_group] == wanted[:, lanes], value, LOWEST)
            kept.append(jnp.max(value.reshape(res_rows // 8, 8, lane_group), axis=0))
        best = kept[0] if groups == 1 else jnp.concatenate(kept, axis=1)
        best_own[block] = jnp.max(jnp.maximum(best, LOWEST), axis=0, keepdims=True)

        @pl.when(n == 0)
        def _():
            best_got[me_s] = best_own[me_s]

        @pl.when(n > 0)
        def _():
            remote(
                best_own.at[block],
                best_got.at[me_s],
                sems.at[BEST, 0],
                sems.at[BEST, 1],
                me_o,
                block,
            ).start()

        @pl.when(n == 1)
        def _():
            x = blocks[pl.ds(PIECES * me_s, PIECES)].reshape(slots, width)
            f = x.astype(F32)
            scale = lax.rsqrt(column_to_row(jnp.sum(f * f, axis=1, keepdims=True)) + EPS)
            mask = jnp.broadcast_to(members[me_s], (clusters, slots)) == (
                iota((clusters, slots), 0) + 1
            ).astype(F32)
            both = held_sums[...] + mm(split_weights(mask, scale), x)
            partial = both[:clusters] + both[clusters:]
            for s in range(splits):
                row, lane = s // chunks_in_row, (s % chunks_in_row) * chunk
                part[s] = partial[row : row + 1, lane : lane + chunk]

            @pl.loop(1, splits)
            def _(i):
                s = other_split(i)
                remote(
                    part.at[s], part_got.at[me_s], sems.at[PART, 0], sems.at[PART, 1], me_o, s
                ).start()

            part_got[me_s] = part[me_s]

        @pl.when(n == min(9, splits - 1))
        def _():
            wait_all(part_got, splits - 1, PART, 1)
            total_own[...] = jnp.sum(part_got[...], axis=0)

            @pl.loop(1, splits)
            def _(i):
                remote(
                    total_own,
                    total.at[me_s],
                    sems.at[TOTAL, 0],
                    sems.at[TOTAL, 1],
                    me_o,
                    other_split(i),
                ).start()

            total[me_s] = total_own[...]

        return carry

    lax.fori_loop(0, splits, score_step, 0)

    wait_all(best_got, splits - 1, BEST, 1)
    best = jnp.max(best_got[...], axis=0)
    for g in range(groups):
        ret_own[g] = best[:, g * lane_group : (g + 1) * lane_group]
    for r in range(owners - 1, 0, -1):
        remote(
            ret_own.at[r // owners_in_group],
            ret_got.at[r],
            sems.at[RET, 0],
            sems.at[RET, 1],
            source_of(r),
            me_s,
        ).start()
    ret_got[0] = ret_own[0]

    wait_all(total, splits - 1, TOTAL, 1)
    for j in range(clusters):
        bits = [total[j * chunks_in_row + i] for i in range(chunks_in_row)]
        v = bits[0] if chunks_in_row == 1 else jnp.concatenate(bits, axis=1)
        cent_ref[j : j + 1] = v * lax.rsqrt(jnp.sum(v * v, axis=1, keepdims=True) + EPS)

    wait_all(send_rows, owners - 1, ROWS, 0)
    wait_all(send_members, owners - 1, MEMBERS, 0)
    wait_all(part, splits - 1, PART, 0)
    wait_all(total, splits - 1, TOTAL, 0)
    wait_all(best_own, splits - 1, BEST, 0)
    for p in range(PIECES + 1):
        for k in range(1, last_major + 1):
            up(me_s, k, p).wait_send()
        for k in range(1, last_minor + 1):
            down(me_s, k, p).wait_send()
        for i in range(ny):
            aside(me_s, i, p).wait_send()

    wait_all(ret_got, owners - 1, RET, 1)
    lane_owner = lax.div(iota((owners, lane_group), 1), cap)
    mine = lane_owner == lax.rem(iota((owners, lane_group), 0), owners_in_group)
    value = jnp.concatenate([ret_got[r] for r in range(owners)], axis=0)
    value = jnp.where(mine, value, 0.0)
    high = value.astype(BF16).astype(F32)
    mid = (value - high).astype(BF16).astype(F32)
    low = value - high - mid
    picked = mm(jnp.concatenate([high, mid, low], axis=0).astype(BF16), place_hot)
    picked = picked[:owners] + picked[owners : 2 * owners] + picked[2 * owners :]
    max_ref[...] = own_scale * jnp.sum(target_hot * picked, axis=0, keepdims=True)
    wait_all(ret_got, owners - 1, RET, 0)


def body(new_rows, cluster_ids, slot_of_cluster, row_counts, resident):
    owners, splits = lax.axis_size("owner"), lax.axis_size("split")
    local, width = new_rows.shape
    clusters = row_counts.shape[2]
    res_rows = resident.shape[2]
    cap = 2 * local // owners
    slots = owners * cap
    lane_group = min(128, slots)
    chunk = clusters * width // splits
    ny = splits // 2
    vmem = pl.BlockSpec(memory_space=pltpu.VMEM)
    hbm = pl.BlockSpec(memory_space=pltpu.HBM)
    dma = pltpu.SemaphoreType.DMA
    major, minor = max(1, ny // 2), max(1, ny // 2 - 1)
    pieces = PIECES + 1
    best, centroids = pl.pallas_call(
        functools.partial(kernel, (owners, splits, local, width, clusters, res_rows, cap)),
        out_shape=(
            jax.ShapeDtypeStruct((1, local), F32),
            jax.ShapeDtypeStruct((clusters, width), F32),
        ),
        in_specs=[hbm] * 5,
        out_specs=(vmem, vmem),
        scratch_shapes=[
            pltpu.VMEM((1, local), I32),
            pltpu.VMEM((1, slot_of_cluster.shape[0]), I32),
            pltpu.SMEM((1, clusters), I32),
            pltpu.VMEM((local, width), BF16),
            pltpu.VMEM((res_rows, width), BF16),
            pltpu.VMEM((res_rows, 128), F32),
            pltpu.VMEM((res_rows, 128), F32),
            pltpu.VMEM((owners, cap, width), BF16),
            pltpu.VMEM((owners, 1, lane_group), F32),
            pltpu.VMEM((owners, cap, width), BF16),
            pltpu.VMEM((owners, 1, lane_group), F32),
            pltpu.VMEM((PIECES * splits, slots // PIECES, width), BF16),
            pltpu.VMEM((splits, 1, slots), F32),
            pltpu.VMEM((2 * clusters, width), F32),
            pltpu.VMEM((splits, 1, chunk), F32),
            pltpu.VMEM((splits, 1, chunk), F32),
            pltpu.VMEM((1, chunk), F32),
            pltpu.VMEM((splits, 1, chunk), F32),
            pltpu.VMEM((splits, 1, slots), F32),
            pltpu.VMEM((splits, 1, slots), F32),
            pltpu.VMEM((slots // lane_group, 1, lane_group), F32),
            pltpu.VMEM((owners, 1, lane_group), F32),
            dma((5,)),
            dma((PIECES,)),
            dma((6, 2)),
            dma((major, pieces)),
            dma((major, pieces)),
            dma((minor, pieces)),
            dma((minor, pieces)),
            dma((ny, pieces)),
            dma((ny, pieces)),
        ],
        compiler_params=pltpu.CompilerParams(
            collective_id=0, has_side_effects=True, vmem_limit_bytes=60 * 1024 * 1024
        ),
        cost_estimate=pl.CostEstimate(
            flops=2 * splits * slots * res_rows * width, bytes_accessed=4 << 20, transcendentals=0
        ),
    )(
        cluster_ids.reshape(1, -1),
        slot_of_cluster.reshape(1, -1),
        row_counts.reshape(1, -1),
        new_rows,
        resident.reshape(res_rows, width),
    )
    return best.reshape(-1), centroids


def solution(mesh):
    placed = (
        P(("owner", "split"), None),
        P(("owner", "split")),
        P(),
        P("owner", "split", None),
        P("owner", "split", None, None),
    )
    return jax.shard_map(
        body,
        mesh=mesh,
        in_specs=placed,
        out_specs=(P(("owner", "split")), P("owner", None)),
        check_vma=False,
    )
```

```python
import functools

import jax
import jax.numpy as jnp
from jax import lax
from jax.experimental import pallas as pl
from jax.experimental.pallas import tpu as pltpu
from jax.sharding import PartitionSpec as P

F32, BF16, I32 = jnp.float32, jnp.bfloat16, jnp.int32
MESH = pl.DeviceIdType.MESH
NT = (((1,), (1,)), ((), ()))
NN = (((1,), (0,)), ((), ()))
EPS = 1e-06
LOWEST = -3.0
PIECES = 4


def iota(shape, dim):
    return lax.broadcasted_iota(I32, shape, dim)


def mm(lhs, rhs, dims=NN):
    return lax.dot_general(lhs, rhs, dims, preferred_element_type=F32)


def column_to_row(column):
    pieces = []
    for start in range(0, column.shape[0], 128):
        piece = column[start : start + 128]
        n = piece.shape[0]
        wide = jnp.broadcast_to(piece, (n, n))
        eye = iota((n, n), 0) == iota((n, n), 1)
        pieces.append(jnp.sum(jnp.where(eye, wide, 0.0), axis=0, keepdims=True))
    return pieces[0] if len(pieces) == 1 else jnp.concatenate(pieces, axis=1)


def split_weights(mask, row):
    high = row.astype(BF16).astype(F32)
    low = row - high
    return jnp.concatenate(
        [jnp.where(mask, high, 0.0), jnp.where(mask, low, 0.0)], axis=0
    ).astype(BF16)


def displacements(owners):
    across = 4 if owners == 32 else 1
    along = owners // across

    def hops(d):
        return min(d[0], across - d[0]) + min(d[1], along - d[1])

    near = sorted(((dx, dz) for dx in range(across) for dz in range(along)), key=hops)
    return across, along, near


def kernel(
    dims,
    ids_hbm,
    table_hbm,
    counts_hbm,
    rows_hbm,
    resident_hbm,
    max_ref,
    cent_ref,
    ids_ref,
    table_ref,
    counts_ref,
    rows_ref,
    held,
    scale_col,
    cluster_col,
    send_rows,
    send_members,
    got_rows,
    got_members,
    blocks,
    members,
    held_sums,
    part,
    part_got,
    total_own,
    total,
    best_own,
    best_got,
    ret_own,
    ret_got,
    load_sems,
    piece_sems,
    sems,
    major_send,
    major_recv,
    minor_send,
    minor_recv,
    sib_send,
    sib_recv,
):
    owners, splits, local, width, clusters, res_rows, cap = dims
    across, along, near = displacements(owners)
    slots = owners * cap
    lane_group = min(128, slots)
    groups = slots // lane_group
    owners_in_group = lane_group // cap
    piece_owners = owners // PIECES
    piece_rows = slots // PIECES
    chunk = clusters * width // splits
    chunks_in_row = width // chunk
    ny = splits // 2
    last_major, last_minor = ny // 2, ny // 2 - 1
    me_o = lax.axis_index("owner")
    me_s = lax.axis_index("split")
    me_x, me_z = me_o // along, me_o % along
    y = me_s // 2
    core = me_s - 2 * y
    step_dir = 1 - 2 * core
    sibling = 2 * y + 1 - core

    def at_y(offset):
        return 2 * ((y + offset * step_dir + 4 * ny) % ny) + core

    def target_of(r):
        dx, dz = near[r]
        return ((me_x + across - dx) % across) * along + (me_z + along - dz) % along

    def source_of(r):
        dx, dz = near[r]
        return ((me_x + dx) % across) * along + (me_z + dz) % along

    def other_split(k):
        return (me_s + k) % splits

    def remote(src, dst, send, recv, owner, split):
        return pltpu.make_async_remote_copy(
            src_ref=src,
            dst_ref=dst,
            send_sem=send,
            recv_sem=recv,
            device_id=(owner, split),
            device_id_type=MESH,
        )

    def wait_piece(piece, sem):
        pltpu.make_async_copy(piece, piece, sem).wait()

    def wait_all(ref, count, kind, side):
        wait_piece(ref.at[pl.ds(0, count)], sems.at[kind, side])

    ROWS, MEMBERS, PART, TOTAL, BEST, RET = range(6)

    loads = [
        pltpu.make_async_copy(src, dst, load_sems.at[i])
        for i, (src, dst) in enumerate(
            (
                (ids_hbm, ids_ref),
                (table_hbm, table_ref),
                (rows_hbm, rows_ref),
                (counts_hbm, counts_ref),
                (resident_hbm, held),
            )
        )
    ]
    barrier = pltpu.get_barrier_semaphore()

    @pl.loop(1, owners)
    def _(k):
        pl.semaphore_signal(
            barrier, inc=1, device_id=((me_o + k) % owners, me_s), device_id_type=MESH
        )

    for load in loads:
        load.start()

    @pl.loop(1, splits)
    def _(k):
        pl.semaphore_signal(
            barrier, inc=1, device_id=(me_o, other_split(k)), device_id_type=MESH
        )

    loads[0].wait()
    loads[1].wait()
    ids = ids_ref[...]
    all_clusters = table_ref.shape[1]
    hot = jnp.where(iota((all_clusters, local), 0) == ids, 1.0, 0.0).astype(BF16)
    table = jnp.broadcast_to(table_ref[...].astype(F32), (8, all_clusters)).astype(BF16)
    slot = mm(table, hot)[0:1].astype(I32)
    target = lax.div(slot, clusters)
    member = slot - target * clusters
    order = iota((owners, local), 0)
    target_of_order = jnp.zeros((owners, local), I32)
    for r in range(owners):
        target_of_order = jnp.where(order == r, target_of(r), target_of_order)
    target_hot = jnp.where(target_of_order == target, 1.0, 0.0)
    rank = jnp.sum(target_hot * order.astype(F32), axis=0, keepdims=True).astype(I32)
    earlier = jnp.where(iota((local, local), 0) < iota((local, local), 1), 1.0, 0.0).astype(BF16)
    before = mm(target_hot.astype(BF16), earlier)
    place = jnp.sum(target_hot * before, axis=0, keepdims=True).astype(I32)
    flat = rank * cap + place
    target_member = (target_hot * (member + 1).astype(F32)).astype(BF16)
    place_hot = jnp.where(
        lax.rem(iota((lane_group, local), 0), cap) == place, 1.0, 0.0
    ).astype(BF16)
    member_rows = mm(target_member, place_hot, NT)
    for r in range(owners):
        send_members[r] = member_rows[r : r + 1]
    loads[2].wait()
    rows = rows_ref[...]
    scatter = jnp.where(iota((slots, local), 0) == flat, 1.0, 0.0).astype(BF16)
    send_rows[...] = mm(scatter, rows).reshape(owners, cap, width).astype(BF16)

    pl.semaphore_wait(barrier, owners + splits - 2)

    for r in range(owners - 1, 0, -1):
        remote(
            send_rows.at[r],
            got_rows.at[r],
            sems.at[ROWS, 0],
            piece_sems.at[r // piece_owners],
            target_of(r),
            me_s,
        ).start()
        remote(
            send_members.at[r],
            got_members.at[r],
            sems.at[MEMBERS, 0],
            sems.at[MEMBERS, 1],
            target_of(r),
            me_s,
        ).start()
    got_rows[0] = send_rows[0]
    got_members[0] = send_members[0]

    floats = rows.astype(F32)
    own_scale = lax.rsqrt(
        column_to_row(jnp.sum(floats * floats, axis=1, keepdims=True)) + EPS
    )
    loads[3].wait()
    loads[4].wait()
    ends = []
    running = counts_ref[0, 0]
    for j in range(clusters):
        ends.append(running)
        if j + 1 < clusters:
            running = running + counts_ref[0, j + 1]
    step_rows = 256

    def cluster_of(index):
        result = jnp.ones(index.shape, I32)
        for end in ends[:-1]:
            result = result + jnp.where(index >= end, 1, 0)
        return result

    def held_step(t, acc):
        start = pl.multiple_of(t * step_rows, step_rows)
        x = held[pl.ds(start, step_rows)]
        f = x.astype(F32)
        scale = lax.rsqrt(jnp.sum(f * f, axis=1, keepdims=True) + EPS)
        scale_col[pl.ds(start, step_rows)] = jnp.broadcast_to(scale, (step_rows, 128))
        cluster_col[pl.ds(start, step_rows)] = cluster_of(
            iota((step_rows, 128), 0) + start
        ).astype(F32)
        row = column_to_row(scale)
        mask = cluster_of(iota((clusters, step_rows), 1) + start) == iota(
            (clusters, step_rows), 0
        ) + 1
        return acc + mm(split_weights(mask, row), x)

    held_sums[...] = lax.fori_loop(
        0, res_rows // step_rows, held_step, jnp.zeros((2 * clusters, width), F32)
    )

    def piece_of(block, p):
        return members.at[block] if p == PIECES else blocks.at[PIECES * block + p]

    def up(block, k, p, hops=1):
        ref = piece_of(block, p)
        return remote(ref, ref, major_send.at[k - 1, p], major_recv.at[k - 1, p], me_o, at_y(hops))

    def down(block, k, p):
        ref = piece_of(block, p)
        return remote(ref, ref, minor_send.at[k - 1, p], minor_recv.at[k - 1, p], me_o, at_y(-1))

    def aside(block, index, p):
        ref = piece_of(block, p)
        return remote(ref, ref, sib_send.at[index, p], sib_recv.at[index, p], me_o, sibling)

    skip = ny == 8

    def skipped(p):
        return skip and p >= PIECES - 1

    def start_own(p):
        up(me_s, 1, p).start()
        if last_minor:
            down(me_s, 1, p).start()
        aside(me_s, 0, p).start()

    for p in range(PIECES):
        first = max(1, p * piece_owners)
        count = (p + 1) * piece_owners - first
        if count:
            wait_piece(got_rows.at[pl.ds(first, count)], piece_sems.at[p])
        blocks[PIECES * me_s + p] = (
            got_rows[pl.ds(p * piece_owners, piece_owners)]
            .astype(F32)
            .reshape(piece_rows, width)
            .astype(BF16)
        )
        start_own(p)
    wait_all(got_members, owners - 1, MEMBERS, 1)
    pieces = []
    for g in range(groups):
        order_of_lane = lax.div(iota((1, lane_group), 1), cap) + g * owners_in_group
        acc = jnp.zeros((1, lane_group), F32)
        for r in range(g * owners_in_group, (g + 1) * owners_in_group):
            acc = acc + jnp.where(order_of_lane == r, got_members[r], 0.0)
        pieces.append(acc)
    members[me_s] = pieces[0] if groups == 1 else jnp.concatenate(pieces, axis=1)
    start_own(PIECES)

    def handle(k, p):
        block = at_y(-k)
        up(block, k, p).wait_recv()
        if not skipped(p):

            @pl.when(k < last_major)
            def _():
                up(block, k + 1, p).start()

        else:

            @pl.when(k < 3)
            def _():
                up(block, k + 1, p).start()

            @pl.when(k == 2)
            def _():
                up(block, 4, p, hops=2).start()

        aside(block, 2 * k - 1, p).start()
        if last_minor:

            @pl.when(k <= last_minor)
            def _():
                block = at_y(k)
                down(block, k, p).wait_recv()

                @pl.when(k < last_minor)
                def _():
                    down(block, k + 1, p).start()

                aside(block, 2 * k, p).start()

    def handle_piece(k, p):
        handle(k, p)
        if p == PIECES - 1:
            handle(k, PIECES)

    def score_step(n, carry):
        k, j = (n + 2) // 4, (n + 2) % 4
        minor, other = j // 2, j % 2
        sign = (1 - 2 * minor) * (1 - 2 * other)
        block = 2 * ((y - sign * k * step_dir + 4 * ny) % ny) + core + other * step_dir

        @pl.when(n == 2)
        def _():
            for p in range(PIECES):
                handle_piece(1, p)

        if last_major > 1:
            t = n - 3
            for p in range(PIECES):

                @pl.when((n >= 3) & (n < 3 + 4 * (last_major - 1)) & (t % 4 == p))
                def _():
                    handle_piece(t // 4 + 2, p)

        @pl.when(other == 1)
        def _():
            for p in range(PIECES + 1):
                aside(block, n // 2, p).wait_recv()

        queries = blocks[pl.ds(PIECES * block, PIECES)].reshape(slots, width)
        wanted = members[block]
        inner = mm(held[...], queries, NT)
        kept = []
        for g in range(groups):
            lanes = slice(g * lane_group, (g + 1) * lane_group)
            value = inner[:, lanes] * scale_col[:, :lane_group]
            value = jnp.where(cluster_col[:, :lane_group] == wanted[:, lanes], value, LOWEST)
            kept.append(jnp.max(value.reshape(res_rows // 8, 8, lane_group), axis=0))
        best = kept[0] if groups == 1 else jnp.concatenate(kept, axis=1)
        best_own[block] = jnp.max(jnp.maximum(best, LOWEST), axis=0, keepdims=True)

        @pl.when(n == 0)
        def _():
            best_got[me_s] = best_own[me_s]

        @pl.when(n > 0)
        def _():
            remote(
                best_own.at[block],
                best_got.at[me_s],
                sems.at[BEST, 0],
                sems.at[BEST, 1],
                me_o,
                block,
            ).start()

        @pl.when(n == 1)
        def _():
            x = blocks[pl.ds(PIECES * me_s, PIECES)].reshape(slots, width)
            f = x.astype(F32)
            scale = lax.rsqrt(column_to_row(jnp.sum(f * f, axis=1, keepdims=True)) + EPS)
            mask = jnp.broadcast_to(members[me_s], (clusters, slots)) == (
                iota((clusters, slots), 0) + 1
            ).astype(F32)
            both = held_sums[...] + mm(split_weights(mask, scale), x)
            partial = both[:clusters] + both[clusters:]
            for s in range(splits):
                row, lane = s // chunks_in_row, (s % chunks_in_row) * chunk
                part[s] = partial[row : row + 1, lane : lane + chunk]

            @pl.loop(1, splits)
            def _(i):
                s = other_split(i)
                remote(
                    part.at[s], part_got.at[me_s], sems.at[PART, 0], sems.at[PART, 1], me_o, s
                ).start()

            part_got[me_s] = part[me_s]

        @pl.when(n == min(9, splits - 1))
        def _():
            wait_all(part_got, splits - 1, PART, 1)
            total_own[...] = jnp.sum(part_got[...], axis=0)

            @pl.loop(1, splits)
            def _(i):
                remote(
                    total_own,
                    total.at[me_s],
                    sems.at[TOTAL, 0],
                    sems.at[TOTAL, 1],
                    me_o,
                    other_split(i),
                ).start()

            total[me_s] = total_own[...]

        return carry

    lax.fori_loop(0, splits, score_step, 0)

    wait_all(best_got, splits - 1, BEST, 1)
    best = jnp.max(best_got[...], axis=0)
    for g in range(groups):
        ret_own[g] = best[:, g * lane_group : (g + 1) * lane_group]
    for r in range(owners - 1, 0, -1):
        remote(
            ret_own.at[r // owners_in_group],
            ret_got.at[r],
            sems.at[RET, 0],
            sems.at[RET, 1],
            source_of(r),
            me_s,
        ).start()
    ret_got[0] = ret_own[0]

    wait_all(total, splits - 1, TOTAL, 1)
    for j in range(clusters):
        bits = [total[j * chunks_in_row + i] for i in range(chunks_in_row)]
        v = bits[0] if chunks_in_row == 1 else jnp.concatenate(bits, axis=1)
        cent_ref[j : j + 1] = v * lax.rsqrt(jnp.sum(v * v, axis=1, keepdims=True) + EPS)

    wait_all(send_rows, owners - 1, ROWS, 0)
    wait_all(send_members, owners - 1, MEMBERS, 0)
    wait_all(part, splits - 1, PART, 0)
    wait_all(total, splits - 1, TOTAL, 0)
    wait_all(best_own, splits - 1, BEST, 0)
    for p in range(PIECES + 1):
        for k in range(1, last_major + 1):
            up(me_s, k, p).wait_send()
        for k in range(1, last_minor + 1):
            down(me_s, k, p).wait_send()
        for i in range(ny):
            aside(me_s, i, p).wait_send()

    wait_all(ret_got, owners - 1, RET, 1)
    lane_owner = lax.div(iota((owners, lane_group), 1), cap)
    mine = lane_owner == lax.rem(iota((owners, lane_group), 0), owners_in_group)
    value = jnp.concatenate([ret_got[r] for r in range(owners)], axis=0)
    value = jnp.where(mine, value, 0.0)
    high = value.astype(BF16).astype(F32)
    mid = (value - high).astype(BF16).astype(F32)
    low = value - high - mid
    picked = mm(jnp.concatenate([high, mid, low], axis=0).astype(BF16), place_hot)
    picked = picked[:owners] + picked[owners : 2 * owners] + picked[2 * owners :]
    max_ref[...] = own_scale * jnp.sum(target_hot * picked, axis=0, keepdims=True)
    wait_all(ret_got, owners - 1, RET, 0)


def body(new_rows, cluster_ids, slot_of_cluster, row_counts, resident):
    owners, splits = lax.axis_size("owner"), lax.axis_size("split")
    local, width = new_rows.shape
    clusters = row_counts.shape[2]
    res_rows = resident.shape[2]
    cap = 2 * local // owners
    slots = owners * cap
    lane_group = min(128, slots)
    chunk = clusters * width // splits
    ny = splits // 2
    vmem = pl.BlockSpec(memory_space=pltpu.VMEM)
    hbm = pl.BlockSpec(memory_space=pltpu.HBM)
    dma = pltpu.SemaphoreType.DMA
    major, minor = max(1, ny // 2), max(1, ny // 2 - 1)
    pieces = PIECES + 1
    best, centroids = pl.pallas_call(
        functools.partial(kernel, (owners, splits, local, width, clusters, res_rows, cap)),
        out_shape=(
            jax.ShapeDtypeStruct((1, local), F32),
            jax.ShapeDtypeStruct((clusters, width), F32),
        ),
        in_specs=[hbm] * 5,
        out_specs=(vmem, vmem),
        scratch_shapes=[
            pltpu.VMEM((1, local), I32),
            pltpu.VMEM((1, slot_of_cluster.shape[0]), I32),
            pltpu.SMEM((1, clusters), I32),
            pltpu.VMEM((local, width), BF16),
            pltpu.VMEM((res_rows, width), BF16),
            pltpu.VMEM((res_rows, 128), F32),
            pltpu.VMEM((res_rows, 128), F32),
            pltpu.VMEM((owners, cap, width), BF16),
            pltpu.VMEM((owners, 1, lane_group), F32),
            pltpu.VMEM((owners, cap, width), BF16),
            pltpu.VMEM((owners, 1, lane_group), F32),
            pltpu.VMEM((PIECES * splits, slots // PIECES, width), BF16),
            pltpu.VMEM((splits, 1, slots), F32),
            pltpu.VMEM((2 * clusters, width), F32),
            pltpu.VMEM((splits, 1, chunk), F32),
            pltpu.VMEM((splits, 1, chunk), F32),
            pltpu.VMEM((1, chunk), F32),
            pltpu.VMEM((splits, 1, chunk), F32),
            pltpu.VMEM((splits, 1, slots), F32),
            pltpu.VMEM((splits, 1, slots), F32),
            pltpu.VMEM((slots // lane_group, 1, lane_group), F32),
            pltpu.VMEM((owners, 1, lane_group), F32),
            dma((5,)),
            dma((PIECES,)),
            dma((6, 2)),
            dma((major, pieces)),
            dma((major, pieces)),
            dma((minor, pieces)),
            dma((minor, pieces)),
            dma((ny, pieces)),
            dma((ny, pieces)),
        ],
        compiler_params=pltpu.CompilerParams(
            collective_id=0, has_side_effects=True, vmem_limit_bytes=48 * 1024 * 1024
        ),
        cost_estimate=pl.CostEstimate(
            flops=2 * splits * slots * res_rows * width, bytes_accessed=4 << 20, transcendentals=0
        ),
    )(
        *(
            pltpu.with_memory_space_constraint(x, pltpu.HBM)
            for x in (
                cluster_ids.reshape(1, -1),
                slot_of_cluster.reshape(1, -1),
                row_counts.reshape(1, -1),
                new_rows,
                resident.reshape(res_rows, width),
            )
        )
    )
    return best.reshape(-1), centroids


def solution(mesh):
    placed = (
        P(("owner", "split"), None),
        P(("owner", "split")),
        P(),
        P("owner", "split", None),
        P("owner", "split", None, None),
    )
    return jax.shard_map(
        body,
        mesh=mesh,
        in_specs=placed,
        out_specs=(P(("owner", "split")), P("owner", None)),
        check_vma=False,
    )
```

```python
import functools

import jax
import jax.numpy as jnp
from jax import lax
from jax.experimental import pallas as pl
from jax.experimental.pallas import tpu as pltpu
from jax.sharding import PartitionSpec as P

F32, BF16, I32 = jnp.float32, jnp.bfloat16, jnp.int32
MESH = pl.DeviceIdType.MESH
NT = (((1,), (1,)), ((), ()))
NN = (((1,), (0,)), ((), ()))
EPS = 1e-06
LOWEST = -3.0
PIECES = 4


def iota(shape, dim):
    return lax.broadcasted_iota(I32, shape, dim)


def mm(lhs, rhs, dims=NN):
    return lax.dot_general(lhs, rhs, dims, preferred_element_type=F32)


def column_to_row(column):
    pieces = []
    for start in range(0, column.shape[0], 128):
        piece = column[start : start + 128]
        n = piece.shape[0]
        wide = jnp.broadcast_to(piece, (n, n))
        eye = iota((n, n), 0) == iota((n, n), 1)
        pieces.append(jnp.sum(jnp.where(eye, wide, 0.0), axis=0, keepdims=True))
    return pieces[0] if len(pieces) == 1 else jnp.concatenate(pieces, axis=1)


def split_weights(mask, row):
    high = row.astype(BF16).astype(F32)
    low = row - high
    return jnp.concatenate(
        [jnp.where(mask, high, 0.0), jnp.where(mask, low, 0.0)], axis=0
    ).astype(BF16)


def displacements(owners):
    across = 4 if owners == 32 else 1
    along = owners // across

    def hops(d):
        return min(d[0], across - d[0]) + min(d[1], along - d[1])

    near = sorted(((dx, dz) for dx in range(across) for dz in range(along)), key=hops)
    return across, along, near


def kernel(
    dims,
    ids_hbm,
    table_hbm,
    counts_hbm,
    rows_hbm,
    resident_hbm,
    max_ref,
    cent_ref,
    ids_ref,
    table_ref,
    counts_ref,
    rows_ref,
    held,
    scale_col,
    cluster_col,
    send_rows,
    send_members,
    got_rows,
    got_members,
    blocks,
    members,
    held_sums,
    part,
    part_got,
    total_own,
    total,
    best_own,
    best_got,
    ret_own,
    ret_got,
    load_sems,
    piece_sems,
    sems,
    major_send,
    major_recv,
    minor_send,
    minor_recv,
    sib_send,
    sib_recv,
):
    owners, splits, local, width, clusters, res_rows, cap = dims
    across, along, near = displacements(owners)
    slots = owners * cap
    lane_group = min(128, slots)
    groups = slots // lane_group
    owners_in_group = lane_group // cap
    piece_owners = owners // PIECES
    piece_rows = slots // PIECES
    chunk = clusters * width // splits
    chunks_in_row = width // chunk
    ny = splits // 2
    last_major, last_minor = ny // 2, ny // 2 - 1
    me_o = lax.axis_index("owner")
    me_s = lax.axis_index("split")
    me_x, me_z = me_o // along, me_o % along
    y = me_s // 2
    core = me_s - 2 * y
    step_dir = 1 - 2 * core
    sibling = 2 * y + 1 - core

    def at_y(offset):
        return 2 * ((y + offset * step_dir + 4 * ny) % ny) + core

    def target_of(r):
        dx, dz = near[r]
        return ((me_x + across - dx) % across) * along + (me_z + along - dz) % along

    def source_of(r):
        dx, dz = near[r]
        return ((me_x + dx) % across) * along + (me_z + dz) % along

    def other_split(k):
        return (me_s + k) % splits

    def remote(src, dst, send, recv, owner, split):
        return pltpu.make_async_remote_copy(
            src_ref=src,
            dst_ref=dst,
            send_sem=send,
            recv_sem=recv,
            device_id=(owner, split),
            device_id_type=MESH,
        )

    def wait_piece(piece, sem):
        pltpu.make_async_copy(piece, piece, sem).wait()

    def wait_all(ref, count, kind, side):
        wait_piece(ref.at[pl.ds(0, count)], sems.at[kind, side])

    ROWS, MEMBERS, PART, TOTAL, BEST, RET = range(6)

    loads = [
        pltpu.make_async_copy(src, dst, load_sems.at[i])
        for i, (src, dst) in enumerate(
            (
                (ids_hbm, ids_ref),
                (table_hbm, table_ref),
                (rows_hbm, rows_ref),
                (counts_hbm, counts_ref),
                (resident_hbm, held),
            )
        )
    ]
    barrier = pltpu.get_barrier_semaphore()

    @pl.loop(1, owners)
    def _(k):
        pl.semaphore_signal(
            barrier, inc=1, device_id=((me_o + k) % owners, me_s), device_id_type=MESH
        )

    for load in loads:
        load.start()

    @pl.loop(1, splits)
    def _(k):
        pl.semaphore_signal(
            barrier, inc=1, device_id=(me_o, other_split(k)), device_id_type=MESH
        )

    loads[0].wait()
    loads[1].wait()
    ids = ids_ref[...]
    all_clusters = table_ref.shape[1]
    hot = jnp.where(iota((all_clusters, local), 0) == ids, 1.0, 0.0).astype(BF16)
    table = jnp.broadcast_to(table_ref[...].astype(F32), (8, all_clusters)).astype(BF16)
    slot = mm(table, hot)[0:1].astype(I32)
    target = lax.div(slot, clusters)
    member = slot - target * clusters
    order = iota((owners, local), 0)
    target_of_order = jnp.zeros((owners, local), I32)
    for r in range(owners):
        target_of_order = jnp.where(order == r, target_of(r), target_of_order)
    target_hot = jnp.where(target_of_order == target, 1.0, 0.0)
    rank = jnp.sum(target_hot * order.astype(F32), axis=0, keepdims=True).astype(I32)
    earlier = jnp.where(iota((local, local), 0) < iota((local, local), 1), 1.0, 0.0).astype(BF16)
    before = mm(target_hot.astype(BF16), earlier)
    place = jnp.sum(target_hot * before, axis=0, keepdims=True).astype(I32)
    flat = rank * cap + place
    target_member = (target_hot * (member + 1).astype(F32)).astype(BF16)
    place_hot = jnp.where(
        lax.rem(iota((lane_group, local), 0), cap) == place, 1.0, 0.0
    ).astype(BF16)
    member_rows = mm(target_member, place_hot, NT)
    for r in range(owners):
        send_members[r] = member_rows[r : r + 1]
    loads[2].wait()
    rows = rows_ref[...]
    scatter = jnp.where(iota((slots, local), 0) == flat, 1.0, 0.0).astype(BF16)
    send_rows[...] = mm(scatter, rows).reshape(owners, cap, width).astype(BF16)

    pl.semaphore_wait(barrier, owners + splits - 2)

    for r in range(owners - 1, 0, -1):
        remote(
            send_rows.at[r],
            got_rows.at[r],
            sems.at[ROWS, 0],
            piece_sems.at[r // piece_owners],
            target_of(r),
            me_s,
        ).start()
        remote(
            send_members.at[r],
            got_members.at[r],
            sems.at[MEMBERS, 0],
            sems.at[MEMBERS, 1],
            target_of(r),
            me_s,
        ).start()
    got_rows[0] = send_rows[0]
    got_members[0] = send_members[0]

    floats = rows.astype(F32)
    own_scale = lax.rsqrt(
        column_to_row(jnp.sum(floats * floats, axis=1, keepdims=True)) + EPS
    )
    loads[3].wait()
    loads[4].wait()
    ends = []
    running = counts_ref[0, 0]
    for j in range(clusters):
        ends.append(running)
        if j + 1 < clusters:
            running = running + counts_ref[0, j + 1]
    step_rows = 256

    def cluster_of(index):
        result = jnp.ones(index.shape, I32)
        for end in ends[:-1]:
            result = result + jnp.where(index >= end, 1, 0)
        return result

    def held_step(t, acc):
        start = pl.multiple_of(t * step_rows, step_rows)
        x = held[pl.ds(start, step_rows)]
        f = x.astype(F32)
        scale = lax.rsqrt(jnp.sum(f * f, axis=1, keepdims=True) + EPS)
        scale_col[pl.ds(start, step_rows)] = jnp.broadcast_to(scale, (step_rows, 128))
        cluster_col[pl.ds(start, step_rows)] = cluster_of(
            iota((step_rows, 128), 0) + start
        ).astype(F32)
        row = column_to_row(scale)
        mask = cluster_of(iota((clusters, step_rows), 1) + start) == iota(
            (clusters, step_rows), 0
        ) + 1
        return acc + mm(split_weights(mask, row), x)

    held_sums[...] = lax.fori_loop(
        0, res_rows // step_rows, held_step, jnp.zeros((2 * clusters, width), F32)
    )

    def piece_of(block, p):
        if isinstance(p, int) and p == PIECES:
            return members.at[block]
        return blocks.at[PIECES * block + p]

    def up(block, k, p):
        ref = piece_of(block, p)
        return remote(ref, ref, major_send.at[k - 1, p], major_recv.at[k - 1, p], me_o, at_y(1))

    def down(block, k, p):
        ref = piece_of(block, p)
        return remote(ref, ref, minor_send.at[k - 1, p], minor_recv.at[k - 1, p], me_o, at_y(-1))

    def aside(block, index, p):
        ref = piece_of(block, p)
        return remote(ref, ref, sib_send.at[index, p], sib_recv.at[index, p], me_o, sibling)

    def start_own(p):
        up(me_s, 1, p).start()
        if last_minor:
            down(me_s, 1, p).start()
        aside(me_s, 0, p).start()

    for p in range(PIECES):
        first = max(1, p * piece_owners)
        count = (p + 1) * piece_owners - first
        if count:
            wait_piece(got_rows.at[pl.ds(first, count)], piece_sems.at[p])
        blocks[PIECES * me_s + p] = (
            got_rows[pl.ds(p * piece_owners, piece_owners)]
            .astype(F32)
            .reshape(piece_rows, width)
            .astype(BF16)
        )
        start_own(p)
    wait_all(got_members, owners - 1, MEMBERS, 1)
    pieces = []
    for g in range(groups):
        order_of_lane = lax.div(iota((1, lane_group), 1), cap) + g * owners_in_group
        acc = jnp.zeros((1, lane_group), F32)
        for r in range(g * owners_in_group, (g + 1) * owners_in_group):
            acc = acc + jnp.where(order_of_lane == r, got_members[r], 0.0)
        pieces.append(acc)
    members[me_s] = pieces[0] if groups == 1 else jnp.concatenate(pieces, axis=1)
    start_own(PIECES)

    def handle(k, p):
        block = at_y(-k)
        up(block, k, p).wait_recv()
        if k < last_major:
            up(block, k + 1, p).start()
        aside(block, 2 * k - 1, p).start()
        if k <= last_minor:
            block = at_y(k)
            down(block, k, p).wait_recv()
            if k < last_minor:
                down(block, k + 1, p).start()
            aside(block, 2 * k, p).start()

    def score(block):
        queries = blocks[pl.ds(PIECES * block, PIECES)].reshape(slots, width)
        wanted = members[block]
        inner = mm(held[...], queries, NT)
        kept = []
        for g in range(groups):
            lanes = slice(g * lane_group, (g + 1) * lane_group)
            value = inner[:, lanes] * scale_col[:, :lane_group]
            value = jnp.where(cluster_col[:, :lane_group] == wanted[:, lanes], value, LOWEST)
            kept.append(jnp.max(value.reshape(res_rows // 8, 8, lane_group), axis=0))
        best = kept[0] if groups == 1 else jnp.concatenate(kept, axis=1)
        best_own[block] = jnp.max(jnp.maximum(best, LOWEST), axis=0, keepdims=True)

    def send_best(block):
        remote(
            best_own.at[block],
            best_got.at[me_s],
            sems.at[BEST, 0],
            sems.at[BEST, 1],
            me_o,
            block,
        ).start()

    def new_sums():
        x = blocks[pl.ds(PIECES * me_s, PIECES)].reshape(slots, width)
        f = x.astype(F32)
        scale = lax.rsqrt(column_to_row(jnp.sum(f * f, axis=1, keepdims=True)) + EPS)
        mask = jnp.broadcast_to(members[me_s], (clusters, slots)) == (
            iota((clusters, slots), 0) + 1
        ).astype(F32)
        both = held_sums[...] + mm(split_weights(mask, scale), x)
        partial = both[:clusters] + both[clusters:]
        for s in range(splits):
            row, lane = s // chunks_in_row, (s % chunks_in_row) * chunk
            part[s] = partial[row : row + 1, lane : lane + chunk]

        @pl.loop(1, splits)
        def _(i):
            s = other_split(i)
            remote(
                part.at[s], part_got.at[me_s], sems.at[PART, 0], sems.at[PART, 1], me_o, s
            ).start()

        part_got[me_s] = part[me_s]

    def share_totals():
        wait_all(part_got, splits - 1, PART, 1)
        total_own[...] = jnp.sum(part_got[...], axis=0)

        @pl.loop(1, splits)
        def _(i):
            remote(
                total_own,
                total.at[me_s],
                sems.at[TOTAL, 0],
                sems.at[TOTAL, 1],
                me_o,
                other_split(i),
            ).start()

        total[me_s] = total_own[...]

    for k in range(last_major + 1):

        @pl.loop(0, 2 if k in (0, last_major) else 4)
        def _(j):
            minor, other = j // 2, j % 2
            sign = (1 - 2 * minor) * (1 - 2 * other)
            block = 2 * ((y - sign * k * step_dir + 4 * ny) % ny) + core + other * step_dir
            index = max(2 * k - 1, 0) + minor

            @pl.when(other == 1)
            def _():
                for p in range(PIECES + 1):
                    aside(block, index, p).wait_recv()

            score(block)
            if k == 0:

                @pl.when(j == 1)
                def _():
                    send_best(block)

            else:
                send_best(block)
            if 0 < k < last_major:
                handle(k + 1, j)

        if k == 0:
            best_got[me_s] = best_own[me_s]
            new_sums()
            for p in range(PIECES):
                handle(1, p)
        if k < last_major:
            handle(k + 1, PIECES)
        if k == last_minor:
            share_totals()

    wait_all(best_got, splits - 1, BEST, 1)
    best = jnp.max(best_got[...], axis=0)
    for g in range(groups):
        ret_own[g] = best[:, g * lane_group : (g + 1) * lane_group]
    for r in range(owners - 1, 0, -1):
        remote(
            ret_own.at[r // owners_in_group],
            ret_got.at[r],
            sems.at[RET, 0],
            sems.at[RET, 1],
            source_of(r),
            me_s,
        ).start()
    ret_got[0] = ret_own[0]

    wait_all(total, splits - 1, TOTAL, 1)
    for j in range(clusters):
        bits = [total[j * chunks_in_row + i] for i in range(chunks_in_row)]
        v = bits[0] if chunks_in_row == 1 else jnp.concatenate(bits, axis=1)
        cent_ref[j : j + 1] = v * lax.rsqrt(jnp.sum(v * v, axis=1, keepdims=True) + EPS)

    wait_all(send_rows, owners - 1, ROWS, 0)
    wait_all(send_members, owners - 1, MEMBERS, 0)
    wait_all(part, splits - 1, PART, 0)
    wait_all(total, splits - 1, TOTAL, 0)
    wait_all(best_own, splits - 1, BEST, 0)
    for p in range(PIECES + 1):
        for k in range(1, last_major + 1):
            up(me_s, k, p).wait_send()
        for k in range(1, last_minor + 1):
            down(me_s, k, p).wait_send()
        for i in range(ny):
            aside(me_s, i, p).wait_send()

    wait_all(ret_got, owners - 1, RET, 1)
    lane_owner = lax.div(iota((owners, lane_group), 1), cap)
    mine = lane_owner == lax.rem(iota((owners, lane_group), 0), owners_in_group)
    value = jnp.concatenate([ret_got[r] for r in range(owners)], axis=0)
    value = jnp.where(mine, value, 0.0)
    high = value.astype(BF16).astype(F32)
    mid = (value - high).astype(BF16).astype(F32)
    low = value - high - mid
    picked = mm(jnp.concatenate([high, mid, low], axis=0).astype(BF16), place_hot)
    picked = picked[:owners] + picked[owners : 2 * owners] + picked[2 * owners :]
    max_ref[...] = own_scale * jnp.sum(target_hot * picked, axis=0, keepdims=True)
    wait_all(ret_got, owners - 1, RET, 0)


def body(new_rows, cluster_ids, slot_of_cluster, row_counts, resident):
    owners, splits = lax.axis_size("owner"), lax.axis_size("split")
    local, width = new_rows.shape
    clusters = row_counts.shape[2]
    res_rows = resident.shape[2]
    cap = 2 * local // owners
    slots = owners * cap
    lane_group = min(128, slots)
    chunk = clusters * width // splits
    ny = splits // 2
    vmem = pl.BlockSpec(memory_space=pltpu.VMEM)
    hbm = pl.BlockSpec(memory_space=pltpu.HBM)
    dma = pltpu.SemaphoreType.DMA
    major, minor = max(1, ny // 2), max(1, ny // 2 - 1)
    pieces = PIECES + 1
    best, centroids = pl.pallas_call(
        functools.partial(kernel, (owners, splits, local, width, clusters, res_rows, cap)),
        out_shape=(
            jax.ShapeDtypeStruct((1, local), F32),
            jax.ShapeDtypeStruct((clusters, width), F32),
        ),
        in_specs=[hbm] * 5,
        out_specs=(vmem, vmem),
        scratch_shapes=[
            pltpu.VMEM((1, local), I32),
            pltpu.VMEM((1, slot_of_cluster.shape[0]), I32),
            pltpu.SMEM((1, clusters), I32),
            pltpu.VMEM((local, width), BF16),
            pltpu.VMEM((res_rows, width), BF16),
            pltpu.VMEM((res_rows, 128), F32),
            pltpu.VMEM((res_rows, 128), F32),
            pltpu.VMEM((owners, cap, width), BF16),
            pltpu.VMEM((owners, 1, lane_group), F32),
            pltpu.VMEM((owners, cap, width), BF16),
            pltpu.VMEM((owners, 1, lane_group), F32),
            pltpu.VMEM((PIECES * splits, slots // PIECES, width), BF16),
            pltpu.VMEM((splits, 1, slots), F32),
            pltpu.VMEM((2 * clusters, width), F32),
            pltpu.VMEM((splits, 1, chunk), F32),
            pltpu.VMEM((splits, 1, chunk), F32),
            pltpu.VMEM((1, chunk), F32),
            pltpu.VMEM((splits, 1, chunk), F32),
            pltpu.VMEM((splits, 1, slots), F32),
            pltpu.VMEM((splits, 1, slots), F32),
            pltpu.VMEM((slots // lane_group, 1, lane_group), F32),
            pltpu.VMEM((owners, 1, lane_group), F32),
            dma((5,)),
            dma((PIECES,)),
            dma((6, 2)),
            dma((major, pieces)),
            dma((major, pieces)),
            dma((minor, pieces)),
            dma((minor, pieces)),
            dma((ny, pieces)),
            dma((ny, pieces)),
        ],
        compiler_params=pltpu.CompilerParams(
            collective_id=0, has_side_effects=True, vmem_limit_bytes=48 * 1024 * 1024
        ),
        cost_estimate=pl.CostEstimate(
            flops=2 * splits * slots * res_rows * width, bytes_accessed=4 << 20, transcendentals=0
        ),
    )(
        *(
            pltpu.with_memory_space_constraint(x, pltpu.HBM)
            for x in (
                cluster_ids.reshape(1, -1),
                slot_of_cluster.reshape(1, -1),
                row_counts.reshape(1, -1),
                new_rows,
                resident.reshape(res_rows, width),
            )
        )
    )
    return best.reshape(-1), centroids


def solution(mesh):
    placed = (
        P(("owner", "split"), None),
        P(("owner", "split")),
        P(),
        P("owner", "split", None),
        P("owner", "split", None, None),
    )
    return jax.shard_map(
        body,
        mesh=mesh,
        in_specs=placed,
        out_specs=(P(("owner", "split")), P("owner", None)),
        check_vma=False,
    )
```

```python
import functools

import jax
import jax.numpy as jnp
from jax import lax
from jax.experimental import pallas as pl
from jax.experimental.pallas import tpu as pltpu
from jax.sharding import PartitionSpec as P

F32, BF16, I32 = jnp.float32, jnp.bfloat16, jnp.int32
MESH = pl.DeviceIdType.MESH
NT = (((1,), (1,)), ((), ()))
NN = (((1,), (0,)), ((), ()))
EPS = 1e-06
LOWEST = -3.0
PIECES = 4


def iota(shape, dim):
    return lax.broadcasted_iota(I32, shape, dim)


def mm(lhs, rhs, dims=NN):
    return lax.dot_general(lhs, rhs, dims, preferred_element_type=F32)


def column_to_row(column):
    pieces = []
    for start in range(0, column.shape[0], 128):
        piece = column[start : start + 128]
        n = piece.shape[0]
        wide = jnp.broadcast_to(piece, (n, n))
        eye = iota((n, n), 0) == iota((n, n), 1)
        pieces.append(jnp.sum(jnp.where(eye, wide, 0.0), axis=0, keepdims=True))
    return pieces[0] if len(pieces) == 1 else jnp.concatenate(pieces, axis=1)


def split_weights(mask, row):
    high = row.astype(BF16).astype(F32)
    low = row - high
    return jnp.concatenate(
        [jnp.where(mask, high, 0.0), jnp.where(mask, low, 0.0)], axis=0
    ).astype(BF16)


def displacements(owners):
    across = 4 if owners == 32 else 1
    along = owners // across

    def hops(d):
        return min(d[0], across - d[0]) + min(d[1], along - d[1])

    near = sorted(((dx, dz) for dx in range(across) for dz in range(along)), key=hops)
    return across, along, near


def kernel(
    dims,
    ids_hbm,
    table_hbm,
    counts_hbm,
    rows_hbm,
    resident_hbm,
    max_ref,
    cent_ref,
    ids_ref,
    table_ref,
    counts_ref,
    rows_ref,
    held,
    scale_col,
    cluster_col,
    send_rows,
    send_members,
    got_rows,
    got_members,
    blocks,
    members,
    held_sums,
    part,
    part_got,
    total_own,
    total,
    best_own,
    best_got,
    ret_own,
    ret_got,
    load_sems,
    piece_sems,
    sems,
    major_send,
    major_recv,
    minor_send,
    minor_recv,
    sib_send,
    sib_recv,
):
    owners, splits, local, width, clusters, res_rows, cap = dims
    across, along, near = displacements(owners)
    slots = owners * cap
    lane_group = min(128, slots)
    groups = slots // lane_group
    owners_in_group = lane_group // cap
    piece_owners = owners // PIECES
    piece_rows = slots // PIECES
    chunk = clusters * width // splits
    chunks_in_row = width // chunk
    ny = splits // 2
    last_major, last_minor = ny // 2, ny // 2 - 1
    me_o = lax.axis_index("owner")
    me_s = lax.axis_index("split")
    me_x, me_z = me_o // along, me_o % along
    y = me_s // 2
    core = me_s - 2 * y
    step_dir = 1 - 2 * core
    sibling = 2 * y + 1 - core

    def at_y(offset):
        return 2 * ((y + offset * step_dir + 4 * ny) % ny) + core

    def target_of(r):
        dx, dz = near[r]
        return ((me_x + across - dx) % across) * along + (me_z + along - dz) % along

    def source_of(r):
        dx, dz = near[r]
        return ((me_x + dx) % across) * along + (me_z + dz) % along

    def other_split(k):
        return (me_s + k) % splits

    def remote(src, dst, send, recv, owner, split):
        return pltpu.make_async_remote_copy(
            src_ref=src,
            dst_ref=dst,
            send_sem=send,
            recv_sem=recv,
            device_id=(owner, split),
            device_id_type=MESH,
        )

    def wait_piece(piece, sem):
        pltpu.make_async_copy(piece, piece, sem).wait()

    def wait_all(ref, count, kind, side):
        wait_piece(ref.at[pl.ds(0, count)], sems.at[kind, side])

    ROWS, MEMBERS, PART, TOTAL, BEST, RET = range(6)

    loads = [
        pltpu.make_async_copy(src, dst, load_sems.at[i])
        for i, (src, dst) in enumerate(
            (
                (ids_hbm, ids_ref),
                (table_hbm, table_ref),
                (rows_hbm, rows_ref),
                (counts_hbm, counts_ref),
                (resident_hbm, held),
            )
        )
    ]
    barrier = pltpu.get_barrier_semaphore()

    @pl.loop(1, owners)
    def _(k):
        pl.semaphore_signal(
            barrier, inc=1, device_id=((me_o + k) % owners, me_s), device_id_type=MESH
        )

    for load in loads:
        load.start()

    @pl.loop(1, splits)
    def _(k):
        pl.semaphore_signal(
            barrier, inc=1, device_id=(me_o, other_split(k)), device_id_type=MESH
        )

    loads[0].wait()
    loads[1].wait()
    ids = ids_ref[...]
    all_clusters = table_ref.shape[1]
    hot = jnp.where(iota((all_clusters, local), 0) == ids, 1.0, 0.0).astype(BF16)
    table = jnp.broadcast_to(table_ref[...].astype(F32), (8, all_clusters)).astype(BF16)
    slot = mm(table, hot)[0:1].astype(I32)
    target = lax.div(slot, clusters)
    member = slot - target * clusters
    order = iota((owners, local), 0)
    target_of_order = jnp.zeros((owners, local), I32)
    for r in range(owners):
        target_of_order = jnp.where(order == r, target_of(r), target_of_order)
    target_hot = jnp.where(target_of_order == target, 1.0, 0.0)
    rank = jnp.sum(target_hot * order.astype(F32), axis=0, keepdims=True).astype(I32)
    earlier = jnp.where(iota((local, local), 0) < iota((local, local), 1), 1.0, 0.0).astype(BF16)
    before = mm(target_hot.astype(BF16), earlier)
    place = jnp.sum(target_hot * before, axis=0, keepdims=True).astype(I32)
    flat = rank * cap + place
    target_member = (target_hot * (member + 1).astype(F32)).astype(BF16)
    place_hot = jnp.where(
        lax.rem(iota((lane_group, local), 0), cap) == place, 1.0, 0.0
    ).astype(BF16)
    member_rows = mm(target_member, place_hot, NT)
    for r in range(owners):
        send_members[r] = member_rows[r : r + 1]
    loads[2].wait()
    rows = rows_ref[...]
    scatter = jnp.where(iota((slots, local), 0) == flat, 1.0, 0.0).astype(BF16)
    send_rows[...] = mm(scatter, rows).reshape(owners, cap, width).astype(BF16)

    pl.semaphore_wait(barrier, owners + splits - 2)

    for r in range(owners - 1, 0, -1):
        remote(
            send_rows.at[r],
            got_rows.at[r],
            sems.at[ROWS, 0],
            piece_sems.at[r // piece_owners],
            target_of(r),
            me_s,
        ).start()
        remote(
            send_members.at[r],
            got_members.at[r],
            sems.at[MEMBERS, 0],
            sems.at[MEMBERS, 1],
            target_of(r),
            me_s,
        ).start()
    got_rows[0] = send_rows[0]
    got_members[0] = send_members[0]

    floats = rows.astype(F32)
    own_scale = lax.rsqrt(
        column_to_row(jnp.sum(floats * floats, axis=1, keepdims=True)) + EPS
    )
    loads[3].wait()
    loads[4].wait()
    ends = []
    running = counts_ref[0, 0]
    for j in range(clusters):
        ends.append(running)
        if j + 1 < clusters:
            running = running + counts_ref[0, j + 1]
    step_rows = 256

    def cluster_of(index):
        result = jnp.ones(index.shape, I32)
        for end in ends[:-1]:
            result = result + jnp.where(index >= end, 1, 0)
        return result

    def held_step(t, acc):
        start = pl.multiple_of(t * step_rows, step_rows)
        x = held[pl.ds(start, step_rows)]
        f = x.astype(F32)
        scale = lax.rsqrt(jnp.sum(f * f, axis=1, keepdims=True) + EPS)
        scale_col[pl.ds(start, step_rows)] = jnp.broadcast_to(scale, (step_rows, 128))
        cluster_col[pl.ds(start, step_rows)] = cluster_of(
            iota((step_rows, 128), 0) + start
        ).astype(F32)
        row = column_to_row(scale)
        mask = cluster_of(iota((clusters, step_rows), 1) + start) == iota(
            (clusters, step_rows), 0
        ) + 1
        return acc + mm(split_weights(mask, row), x)

    held_sums[...] = lax.fori_loop(
        0, res_rows // step_rows, held_step, jnp.zeros((2 * clusters, width), F32)
    )

    def piece_of(block, p):
        if isinstance(p, int) and p == PIECES:
            return members.at[block]
        return blocks.at[PIECES * block + p]

    def up(block, k, p):
        ref = piece_of(block, p)
        return remote(ref, ref, major_send.at[k - 1, p], major_recv.at[k - 1, p], me_o, at_y(1))

    def down(block, k, p):
        ref = piece_of(block, p)
        return remote(ref, ref, minor_send.at[k - 1, p], minor_recv.at[k - 1, p], me_o, at_y(-1))

    def aside(block, index, p):
        ref = piece_of(block, p)
        return remote(ref, ref, sib_send.at[index, p], sib_recv.at[index, p], me_o, sibling)

    def start_own(p):
        up(me_s, 1, p).start()
        if last_minor:
            down(me_s, 1, p).start()
        aside(me_s, 0, p).start()

    for p in range(PIECES):
        first = max(1, p * piece_owners)
        count = (p + 1) * piece_owners - first
        if count:
            wait_piece(got_rows.at[pl.ds(first, count)], piece_sems.at[p])
        blocks[PIECES * me_s + p] = (
            got_rows[pl.ds(p * piece_owners, piece_owners)]
            .astype(F32)
            .reshape(piece_rows, width)
            .astype(BF16)
        )
        start_own(p)
    wait_all(got_members, owners - 1, MEMBERS, 1)
    pieces = []
    for g in range(groups):
        order_of_lane = lax.div(iota((1, lane_group), 1), cap) + g * owners_in_group
        acc = jnp.zeros((1, lane_group), F32)
        for r in range(g * owners_in_group, (g + 1) * owners_in_group):
            acc = acc + jnp.where(order_of_lane == r, got_members[r], 0.0)
        pieces.append(acc)
    members[me_s] = pieces[0] if groups == 1 else jnp.concatenate(pieces, axis=1)
    start_own(PIECES)

    def handle(k, p):
        block = at_y(-k)
        up(block, k, p).wait_recv()
        if k < last_major:
            up(block, k + 1, p).start()
        aside(block, 2 * k - 1, p).start()
        if k <= last_minor:
            block = at_y(k)
            down(block, k, p).wait_recv()
            if k < last_minor:
                down(block, k + 1, p).start()
            aside(block, 2 * k, p).start()

    def score(block):
        queries = blocks[pl.ds(PIECES * block, PIECES)].reshape(slots, width)
        wanted = members[block]
        inner = mm(held[...], queries, NT)
        kept = []
        for g in range(groups):
            lanes = slice(g * lane_group, (g + 1) * lane_group)
            value = inner[:, lanes] * scale_col[:, :lane_group]
            value = jnp.where(cluster_col[:, :lane_group] == wanted[:, lanes], value, LOWEST)
            kept.append(jnp.max(value.reshape(res_rows // 8, 8, lane_group), axis=0))
        best = kept[0] if groups == 1 else jnp.concatenate(kept, axis=1)
        best_own[block] = jnp.max(jnp.maximum(best, LOWEST), axis=0, keepdims=True)

    def send_best(block):
        remote(
            best_own.at[block],
            best_got.at[me_s],
            sems.at[BEST, 0],
            sems.at[BEST, 1],
            me_o,
            block,
        ).start()

    def new_sums():
        x = blocks[pl.ds(PIECES * me_s, PIECES)].reshape(slots, width)
        f = x.astype(F32)
        scale = lax.rsqrt(column_to_row(jnp.sum(f * f, axis=1, keepdims=True)) + EPS)
        mask = jnp.broadcast_to(members[me_s], (clusters, slots)) == (
            iota((clusters, slots), 0) + 1
        ).astype(F32)
        both = held_sums[...] + mm(split_weights(mask, scale), x)
        partial = both[:clusters] + both[clusters:]
        for s in range(splits):
            row, lane = s // chunks_in_row, (s % chunks_in_row) * chunk
            part[s] = partial[row : row + 1, lane : lane + chunk]

        @pl.loop(1, splits)
        def _(i):
            s = other_split(i)
            remote(
                part.at[s], part_got.at[me_s], sems.at[PART, 0], sems.at[PART, 1], me_o, s
            ).start()

        part_got[me_s] = part[me_s]

    def share_totals():
        wait_all(part_got, splits - 1, PART, 1)
        total_own[...] = jnp.sum(part_got[...], axis=0)

        @pl.loop(1, splits)
        def _(i):
            remote(
                total_own,
                total.at[me_s],
                sems.at[TOTAL, 0],
                sems.at[TOTAL, 1],
                me_o,
                other_split(i),
            ).start()

        total[me_s] = total_own[...]

    for k in range(last_major + 1):

        @pl.loop(0, 2 if k in (0, last_major) else 4)
        def _(j):
            minor, other = j // 2, j % 2
            sign = (1 - 2 * minor) * (1 - 2 * other)
            block = 2 * ((y - sign * k * step_dir + 4 * ny) % ny) + core + other * step_dir
            index = max(2 * k - 1, 0) + minor

            @pl.when(other == 1)
            def _():
                for p in range(PIECES + 1):
                    aside(block, index, p).wait_recv()

            score(block)
            if k == 0:

                @pl.when(j == 1)
                def _():
                    send_best(block)

            else:
                send_best(block)
            if 0 < k < last_major:
                handle(k + 1, j)

        if k == 0:
            best_got[me_s] = best_own[me_s]
            new_sums()
            for p in range(PIECES):
                handle(1, p)
        if k < last_major:
            handle(k + 1, PIECES)
        if k == last_major:
            share_totals()

    wait_all(best_got, splits - 1, BEST, 1)
    best = jnp.max(best_got[...], axis=0)
    for g in range(groups):
        ret_own[g] = best[:, g * lane_group : (g + 1) * lane_group]
    for r in range(owners - 1, 0, -1):
        remote(
            ret_own.at[r // owners_in_group],
            ret_got.at[r],
            sems.at[RET, 0],
            sems.at[RET, 1],
            source_of(r),
            me_s,
        ).start()
    ret_got[0] = ret_own[0]

    wait_all(total, splits - 1, TOTAL, 1)
    for j in range(clusters):
        bits = [total[j * chunks_in_row + i] for i in range(chunks_in_row)]
        v = bits[0] if chunks_in_row == 1 else jnp.concatenate(bits, axis=1)
        cent_ref[j : j + 1] = v * lax.rsqrt(jnp.sum(v * v, axis=1, keepdims=True) + EPS)

    wait_all(send_rows, owners - 1, ROWS, 0)
    wait_all(send_members, owners - 1, MEMBERS, 0)
    wait_all(part, splits - 1, PART, 0)
    wait_all(total, splits - 1, TOTAL, 0)
    wait_all(best_own, splits - 1, BEST, 0)
    for p in range(PIECES + 1):
        for k in range(1, last_major + 1):
            up(me_s, k, p).wait_send()
        for k in range(1, last_minor + 1):
            down(me_s, k, p).wait_send()
        for i in range(ny):
            aside(me_s, i, p).wait_send()

    wait_all(ret_got, owners - 1, RET, 1)
    lane_owner = lax.div(iota((owners, lane_group), 1), cap)
    mine = lane_owner == lax.rem(iota((owners, lane_group), 0), owners_in_group)
    value = jnp.concatenate([ret_got[r] for r in range(owners)], axis=0)
    value = jnp.where(mine, value, 0.0)
    high = value.astype(BF16).astype(F32)
    mid = (value - high).astype(BF16).astype(F32)
    low = value - high - mid
    picked = mm(jnp.concatenate([high, mid, low], axis=0).astype(BF16), place_hot)
    picked = picked[:owners] + picked[owners : 2 * owners] + picked[2 * owners :]
    max_ref[...] = own_scale * jnp.sum(target_hot * picked, axis=0, keepdims=True)
    wait_all(ret_got, owners - 1, RET, 0)


def body(new_rows, cluster_ids, slot_of_cluster, row_counts, resident):
    owners, splits = lax.axis_size("owner"), lax.axis_size("split")
    local, width = new_rows.shape
    clusters = row_counts.shape[2]
    res_rows = resident.shape[2]
    cap = 2 * local // owners
    slots = owners * cap
    lane_group = min(128, slots)
    chunk = clusters * width // splits
    ny = splits // 2
    vmem = pl.BlockSpec(memory_space=pltpu.VMEM)
    hbm = pl.BlockSpec(memory_space=pltpu.HBM)
    dma = pltpu.SemaphoreType.DMA
    major, minor = max(1, ny // 2), max(1, ny // 2 - 1)
    pieces = PIECES + 1
    best, centroids = pl.pallas_call(
        functools.partial(kernel, (owners, splits, local, width, clusters, res_rows, cap)),
        out_shape=(
            jax.ShapeDtypeStruct((1, local), F32),
            jax.ShapeDtypeStruct((clusters, width), F32),
        ),
        in_specs=[hbm] * 5,
        out_specs=(vmem, vmem),
        scratch_shapes=[
            pltpu.VMEM((1, local), I32),
            pltpu.VMEM((1, slot_of_cluster.shape[0]), I32),
            pltpu.SMEM((1, clusters), I32),
            pltpu.VMEM((local, width), BF16),
            pltpu.VMEM((res_rows, width), BF16),
            pltpu.VMEM((res_rows, 128), F32),
            pltpu.VMEM((res_rows, 128), F32),
            pltpu.VMEM((owners, cap, width), BF16),
            pltpu.VMEM((owners, 1, lane_group), F32),
            pltpu.VMEM((owners, cap, width), BF16),
            pltpu.VMEM((owners, 1, lane_group), F32),
            pltpu.VMEM((PIECES * splits, slots // PIECES, width), BF16),
            pltpu.VMEM((splits, 1, slots), F32),
            pltpu.VMEM((2 * clusters, width), F32),
            pltpu.VMEM((splits, 1, chunk), F32),
            pltpu.VMEM((splits, 1, chunk), F32),
            pltpu.VMEM((1, chunk), F32),
            pltpu.VMEM((splits, 1, chunk), F32),
            pltpu.VMEM((splits, 1, slots), F32),
            pltpu.VMEM((splits, 1, slots), F32),
            pltpu.VMEM((slots // lane_group, 1, lane_group), F32),
            pltpu.VMEM((owners, 1, lane_group), F32),
            dma((5,)),
            dma((PIECES,)),
            dma((6, 2)),
            dma((major, pieces)),
            dma((major, pieces)),
            dma((minor, pieces)),
            dma((minor, pieces)),
            dma((ny, pieces)),
            dma((ny, pieces)),
        ],
        compiler_params=pltpu.CompilerParams(
            collective_id=0, has_side_effects=True, vmem_limit_bytes=48 * 1024 * 1024
        ),
        cost_estimate=pl.CostEstimate(
            flops=2 * splits * slots * res_rows * width, bytes_accessed=4 << 20, transcendentals=0
        ),
    )(
        *(
            pltpu.with_memory_space_constraint(x, pltpu.HBM)
            for x in (
                cluster_ids.reshape(1, -1),
                slot_of_cluster.reshape(1, -1),
                row_counts.reshape(1, -1),
                new_rows,
                resident.reshape(res_rows, width),
            )
        )
    )
    return best.reshape(-1), centroids


def solution(mesh):
    placed = (
        P(("owner", "split"), None),
        P(("owner", "split")),
        P(),
        P("owner", "split", None),
        P("owner", "split", None, None),
    )
    return jax.shard_map(
        body,
        mesh=mesh,
        in_specs=placed,
        out_specs=(P(("owner", "split")), P("owner", None)),
        check_vma=False,
    )
```
